256 devices in a mesh: freq: 32 (over z_lo, y, x), band: 8 (over z_hi, core).
Axes of the slice: x: 4, y: 4, z: 8 (z_hi: 4, z_lo: 2; z = z_hi * 2 + z_lo), core: 2. Of those that a mesh axis runs over, the one named last changes fastest.
Arguments:
- wavefields: float32 [32, 4, 1024, 1024], P('freq', None, None, 'band'), may hold values from -6 to 6
- slowness_store: float32 [32, 1024, 1024], P('freq', None, 'band'), may hold values from 0.8 to 1.25
- owner_plan: int32 [3], replicated, may hold values from 0 to 31
- freq_slot: int32 [32], P('freq'), may hold values from 0 to 31, as said below
Outputs:
- migrated_image: float32 [3, 1024, 1024], P(None, 'freq', 'band')
- bottom_fields: float32 [32, 4, 1024, 1024], P('freq', None, None, 'band')
The draws below stay inside these ranges and needn't reach their ends.
Inputs may be any that keep to these rules, and one draw needn't show every extreme that they name: `freq_slot`: every frequency number appears once.
All inputs are finite; a program needn't handle non-finite values.
Results may differ from the reference program's by a relative error of at most 0.034.
Values may be sent and summed in bfloat16 or wider, within the bound.
A program may use at most 128 MiB of HBM per device.

```python
import math
import jax
import jax.numpy as jnp
from jax import lax

NX = 1024
NZ = 3
FREQS = 32
NY = 1024


OMEGA_LO = 1.5


OMEGA_HI = 3.0


def frequency_order(key):
    return jax.random.permutation(jax.random.fold_in(key, 911), FREQS).astype(jnp.int32)


def draw_freq_slot(key, part):
    return frequency_order(key)


def draw_wavefields(key, part):
    order = frequency_order(key)
    key = jax.random.fold_in(key, 3)
    omega_values = OMEGA_LO + (OMEGA_HI - OMEGA_LO) * (order.astype(jnp.float32) + 0.5) / FREQS
    noise_key = jax.random.fold_in(key, 17)
    mode_key = jax.random.fold_in(key, 29)
    column_pos = jnp.arange(1, NY + 1, dtype=jnp.float32)
    row_pos = jnp.arange(1, NX + 1, dtype=jnp.int32)
    total = jnp.clip(jax.random.normal(noise_key, (FREQS, 4, NX, NY), jnp.float32), -2.4, 2.4)
    strength = 1.2
    limit = max(NX // 3, 1)
    for mode_index in range(3):
        sub_key = jax.random.fold_in(mode_key, mode_index)
        row_index = jax.random.randint(jax.random.fold_in(sub_key, 0), (FREQS,), 0, limit)
        margin = jax.random.uniform(jax.random.fold_in(sub_key, 1), (FREQS,), jnp.float32, 0.002, 0.02)
        weights = jax.random.uniform(jax.random.fold_in(sub_key, 2), (FREQS, 4), jnp.float32, -strength, strength)
        wave_x = math.pi * (row_index + 1).astype(jnp.float32) / (NX + 1)
        wave_y = jnp.sqrt(jnp.maximum(omega_values * omega_values - wave_x * wave_x, 0.0)) - margin
        modulo = (row_index + 1)[:, None] * row_pos[None, :] % (2 * (NX + 1))
        along_x = jnp.sin(math.pi * modulo.astype(jnp.float32) / (NX + 1))
        along_y = jnp.sin(wave_y[:, None] * column_pos[None, :])
        total = total + weights[:, :, None, None] * along_x[:, None, :, None] * along_y[:, None, None, :]
    return total


def shard_levels(own_key, extent, cuts, low, largest):
    def one(dim, blocks):
        draws = jax.random.uniform(jax.random.fold_in(jax.random.fold_in(own_key, 6), dim), (blocks,), jnp.float32, low / len(cuts), largest / len(cuts))
        return jnp.repeat(jnp.exp(draws), extent[dim] // blocks).reshape((-1,) + (1,) * (len(extent) - dim - 1))

    gain = one(*cuts[0])
    for cut in cuts[1:]:
        gain = gain * one(*cut)
    return gain


def setup_inputs(seed: int = 0) -> dict:
    key_list = jax.random.split(jax.random.key(seed), 5)
    return {
        "wavefields": draw_wavefields(jax.random.fold_in(key_list[4], 71), 0),
        "slowness_store": jnp.clip(0.8 + 0.45 * jax.random.uniform(key_list[1], (FREQS, NX, NY), jnp.float32) ** shard_levels(key_list[1], (FREQS, NX, NY), ((0, 32), (2, 8)), -0.2, 0.2), 0.8, 1.25),
        "owner_plan": jax.random.randint(key_list[2], (NZ,), 0, FREQS).astype(jnp.int32),
        "freq_slot": draw_freq_slot(jax.random.fold_in(key_list[4], 71), 0),
    }


OMEGA_LO = 1.5
OMEGA_HI = 3.0

def sine_table(length):
    ordinal = jnp.arange(1, length + 1, dtype=jnp.int32)
    modulo = ordinal[:, None] * ordinal[None, :] % (2 * (length + 1))
    angles = math.pi * modulo.astype(jnp.float32) / (length + 1)
    return (math.sqrt(2.0 / (length + 1)) * jnp.sin(angles)).astype(jnp.bfloat16)

def wavenumbers(length, first, total):
    ordinal = first + jnp.arange(1, length + 1, dtype=jnp.int32)
    return math.pi * ordinal.astype(jnp.float32) / (total + 1)

def spectral_factors(omega_value, wave_rows, wave_columns):
    squared = omega_value * omega_value - wave_rows[:, None] * wave_rows[:, None] - wave_columns[None, :] * wave_columns[None, :]
    vertical = jnp.sqrt(jnp.maximum(squared, 0.0))
    decay = jnp.sqrt(jnp.maximum(-squared, 0.0))
    return (jnp.cos(vertical), jnp.sin(vertical), jnp.exp(-decay))

def rotate(fields, cosine, sine_part, damping):
    pieces = []
    for offset, handed in ((0, -1.0), (2, 1.0)):
        real_part = fields[offset]
        imag_part = fields[offset + 1]
        pieces.append(damping * (real_part * cosine - handed * imag_part * sine_part))
        pieces.append(damping * (imag_part * cosine + handed * real_part * sine_part))
    return jnp.stack(pieces)

def reference(wavefields, slowness_store, owner_plan, freq_slot):
    lateral_table = sine_table(NX).astype(jnp.float32)
    band_table = sine_table(NY).astype(jnp.float32)
    wave_rows = wavenumbers(NX, 0, NX)
    wave_columns = wavenumbers(NY, 0, NY)
    normalizer = 1.0 / math.sqrt(FREQS)
    slab_list = [slowness_store[owner_plan[layer_index]] for layer_index in range(NZ)]
    omegas = OMEGA_LO + (OMEGA_HI - OMEGA_LO) * (freq_slot.astype(jnp.float32) + 0.5) / FREQS

    def one_frequency(image_sum, inputs):
        fields, omega_value = inputs
        cosine_k, sine_k, damping_k = spectral_factors(omega_value, wave_rows, wave_columns)
        layers = []
        for layer_index in range(NZ):
            split_phase = omega_value * (slab_list[layer_index] - 1.0)
            shifted = rotate(fields, jnp.cos(split_phase), jnp.sin(split_phase), 1.0).astype(jnp.bfloat16)
            half_spectrum = jnp.einsum('kx,cxy->cky', lateral_table, shifted.astype(jnp.float32)).astype(jnp.bfloat16)
            spectrum = jnp.einsum('cky,ly->ckl', half_spectrum.astype(jnp.float32), band_table)
            turned = rotate(spectrum, cosine_k, sine_k, damping_k).astype(jnp.bfloat16)
            partial_back = jnp.einsum('ckl,ly->cky', turned.astype(jnp.float32), band_table).astype(jnp.bfloat16)
            fields = jnp.einsum('kx,cky->cxy', lateral_table, partial_back.astype(jnp.float32))
            layers.append((fields[0] * fields[2] + fields[1] * fields[3]) * normalizer)
        return (image_sum + jnp.stack(layers), fields)
    image_sum, bottom = lax.scan(one_frequency, jnp.zeros((NZ, NX, NY), jnp.float32), (wavefields, omegas))
    return (image_sum, bottom)
```

```python
import functools
import math

import jax
import jax.numpy as jnp
import numpy as np
from jax import lax
from jax.experimental import pallas as pl
from jax.experimental.pallas import tpu as pltpu
from jax.sharding import PartitionSpec as P

OMEGA_LO = 1.5
OMEGA_HI = 3.0
MESH = pl.DeviceIdType.MESH
BF16 = jnp.bfloat16
F32 = jnp.float32


def sine_table(length):
    ordinal = np.arange(1, length + 1, dtype=np.int64)
    modulo = ordinal[:, None] * ordinal[None, :] % (2 * (length + 1))
    angles = math.pi * modulo / (length + 1)
    return (math.sqrt(2.0 / (length + 1)) * np.sin(angles)).astype(np.float32).astype(BF16)


def small_cos_sin(phi):
    p2 = phi * phi
    cosine = 1.0 + p2 * (-1 / 2 + p2 * (1 / 24 + p2 * (-1 / 720 + p2 * (1 / 40320))))
    sine = phi * (1.0 + p2 * (-1 / 6 + p2 * (1 / 120 + p2 * (-1 / 5040 + p2 * (1 / 362880)))))
    return cosine, sine


def kernel(
    dims,
    owner,
    slot,
    table,
    slab,
    wave,
    image,
    bottom,
    fields,
    shifted,
    tx,
    rx,
    turned,
    ptx,
    prx,
    trig,
    factor,
    chunk_tx,
    chunk_rx,
    select,
    slow,
    image_tx,
    image_rx,
    load_sem,
    chunk_send,
    chunk_recv,
    slow_send,
    slow_recv,
    fwd_send,
    fwd_recv,
    back_send,
    back_recv,
    image_send,
    image_recv,
):
    freqs, bands, lateral, depth = dims
    strip = lateral // bands
    rows = lateral // freqs
    tile = min(256, lateral)
    tiles = lateral // tile
    per_tile = tile // strip
    f = lax.axis_index("freq")
    b = lax.axis_index("band")
    omega = OMEGA_LO + (OMEGA_HI - OMEGA_LO) * (slot[0].astype(F32) + 0.5) / freqs

    def wait_bytes(ref, sem):
        pltpu.make_async_copy(ref, ref, sem).wait()

    barrier = pltpu.get_barrier_semaphore()

    def greet_freq(d, carry):
        pl.semaphore_signal(
            barrier, inc=1, device_id={"freq": lax.rem(f + d, freqs)}, device_id_type=MESH
        )
        return carry

    def greet_band(d, carry):
        pl.semaphore_signal(
            barrier, inc=1, device_id={"band": lax.rem(b + d, bands)}, device_id_type=MESH
        )
        return carry

    lax.fori_loop(1, freqs, greet_freq, 0)
    lax.fori_loop(1, bands, greet_band, 0)
    loads = [
        pltpu.make_async_copy(
            wave.at[0, 2 * u + c], fields.at[u, :, pl.ds(c * strip, strip)], load_sem
        )
        for u in range(2)
        for c in range(2)
    ]
    for load in loads:
        load.start()
    chunk_tx[:, 0:rows, :] = (slab[0] - 1.0).astype(BF16).reshape(freqs, rows, strip)
    chunk_tx[:, rows:, :] = jnp.full((freqs, 16, strip), slot[0].astype(F32)).astype(BF16)
    pl.semaphore_wait(barrier, freqs + bands - 2)

    def send_chunk(d, carry):
        g = lax.rem(f + d, freqs)
        pltpu.make_async_remote_copy(
            chunk_tx.at[g],
            chunk_rx.at[f],
            chunk_send,
            chunk_recv,
            device_id={"freq": g},
            device_id_type=MESH,
        ).start()
        return carry

    lax.fori_loop(1, freqs, send_chunk, 0)
    pltpu.make_async_copy(chunk_tx.at[f], chunk_rx.at[f], chunk_recv).start()

    def make_factor(n, carry):
        lanes = pl.ds(pl.multiple_of(n * strip, strip), strip)
        shape = (strip, strip)
        kx = (lax.broadcasted_iota(jnp.int32, shape, 0) + (b * strip + 1)).astype(F32)
        ky = (lax.broadcasted_iota(jnp.int32, shape, 1) + (n * strip + 1)).astype(F32)
        kx = math.pi * kx / (lateral + 1)
        ky = math.pi * ky / (lateral + 1)
        q = omega * omega - kx * kx - ky * ky
        theta = jnp.sqrt(jnp.maximum(q, 0.0))
        damp = jnp.exp(-jnp.sqrt(jnp.maximum(-q, 0.0)))
        factor[0, :, lanes] = damp * jnp.cos(theta)
        factor[1, :, lanes] = damp * jnp.sin(theta)
        return carry

    lax.fori_loop(0, bands, make_factor, 0)

    wait_bytes(chunk_rx, chunk_recv)
    for z in range(depth):
        select[z] = chunk_rx[owner[z], 0:rows, :]

    def send_slow(first, count, sem):
        def body(d, carry):
            g = lax.rem(f + d, freqs)
            pltpu.make_async_remote_copy(
                select.at[pl.ds(first, count)],
                slow.at[pl.ds(first, count), f],
                slow_send.at[sem],
                slow_recv.at[sem],
                device_id={"freq": g},
                device_id_type=MESH,
            ).start()
            return carry

        lax.fori_loop(1, freqs, body, 0)
        pltpu.make_async_copy(
            select.at[pl.ds(first, count)], slow.at[pl.ds(first, count), f], slow_recv.at[sem]
        ).start()

    def make_trig(z):
        def body(g, carry):
            block = pl.ds(pl.multiple_of(g * rows, rows), rows)
            cosine, sine = small_cos_sin(omega * slow[z, g].astype(F32))
            trig[z, 0, block] = cosine
            trig[z, 1, block] = sine
            return carry

        lax.fori_loop(0, freqs, body, 0)

    send_slow(0, 1, 0)
    send_slow(1, depth - 1, 1)
    for load in loads:
        load.wait()
    wait_bytes(slow.at[0], slow_recv.at[0])
    make_trig(0)

    def hand(u):
        return -1.0 if u == 0 else 1.0

    def to_wavenumbers(z, u):
        def shift(i, carry):
            block = pl.ds(pl.multiple_of(i * strip, strip), strip)
            cosine = trig[z, 0, block]
            sine = trig[z, 1, block] * hand(u)
            re = fields[u, block, 0:strip]
            im = fields[u, block, strip:]
            shifted[u, block, 0:strip] = (re * cosine - im * sine).astype(BF16)
            shifted[u, block, strip:] = (im * cosine + re * sine).astype(BF16)
            return carry

        lax.fori_loop(0, bands, shift, 0)

        @pl.when(z > 0)
        def _():
            wait_bytes(tx.at[u, :, pl.ds(0, lateral - strip)], fwd_send.at[u])

        def product(i, carry):
            t = lax.rem(b // per_tile + 1 + i, tiles)
            block = pl.ds(pl.multiple_of(t * tile, tile), tile)
            half = jnp.dot(table[block, :], shifted[u], preferred_element_type=F32).astype(BF16)
            tx[u, 0, block] = half[:, 0:strip]
            tx[u, 1, block] = half[:, strip:]
            for p in range(per_tile):
                j = t * per_tile + p
                src = tx.at[u, :, pl.ds(pl.multiple_of(j * strip, strip), strip)]
                dst = rx.at[u, :, :, pl.ds(pl.multiple_of(b * strip, strip), strip)]

                @pl.when(j != b)
                def _():
                    pltpu.make_async_remote_copy(
                        src,
                        dst,
                        fwd_send.at[u],
                        fwd_recv.at[u],
                        device_id={"band": j},
                        device_id_type=MESH,
                    ).start()

                @pl.when(j == b)
                def _():
                    pltpu.make_async_copy(src, dst, fwd_recv.at[u]).start()

            return carry

        lax.fori_loop(0, tiles, product, 0)

    def turn(z, u):
        wait_bytes(rx.at[u], fwd_recv.at[u])

        def product(n, carry):
            lanes = pl.ds(pl.multiple_of(n * tile, tile), tile)
            lines = rx[u].reshape(2 * strip, lateral)
            spectrum = jnp.dot(lines, table[:, lanes], preferred_element_type=F32)
            re = spectrum[0:strip]
            im = spectrum[strip:]
            cosine = factor[0, :, lanes]
            sine = factor[1, :, lanes] * hand(u)
            turned[u, 0:strip, lanes] = (re * cosine - im * sine).astype(BF16)
            turned[u, strip:, lanes] = (im * cosine + re * sine).astype(BF16)
            return carry

        lax.fori_loop(0, tiles, product, 0)

        @pl.when(z > 0)
        def _():
            wait_bytes(ptx.at[u, pl.ds(0, bands - 1)], back_send.at[u])

        def back(i, carry):
            t = lax.rem(b // per_tile + 1 + i, tiles)
            lanes = pl.ds(pl.multiple_of(t * tile, tile), tile)
            partial = jnp.dot(turned[u], table[:, lanes], preferred_element_type=F32).astype(BF16)
            for p in range(per_tile):
                j = t * per_tile + p
                cols = slice(p * strip, (p + 1) * strip)
                ptx[u, j, :, 0:strip] = partial[0:strip, cols]
                ptx[u, j, :, strip:] = partial[strip:, cols]
                src = ptx.at[u, j]
                dst = prx.at[u, pl.ds(pl.multiple_of(b * strip, strip), strip)]

                @pl.when(j != b)
                def _():
                    pltpu.make_async_remote_copy(
                        src,
                        dst,
                        back_send.at[u],
                        back_recv.at[u],
                        device_id={"band": j},
                        device_id_type=MESH,
                    ).start()

                @pl.when(j == b)
                def _():
                    pltpu.make_async_copy(src, dst, back_recv.at[u]).start()

            return carry

        lax.fori_loop(0, tiles, back, 0)

    def to_fields(u):
        wait_bytes(prx.at[u], back_recv.at[u])

        def product(i, carry):
            block = pl.ds(pl.multiple_of(i * tile, tile), tile)
            fields[u, block] = jnp.dot(table[block, :], prx[u], preferred_element_type=F32)
            return carry

        lax.fori_loop(0, tiles, product, 0)

    normalizer = 1.0 / math.sqrt(freqs)

    def send_image(z):
        def term(i, carry):
            block = pl.ds(pl.multiple_of(i * strip, strip), strip)
            value = fields[0, block] * fields[1, block]
            value = (value[:, 0:strip] + value[:, strip:]) * normalizer
            image_tx[z, block] = value.astype(BF16)
            return carry

        lax.fori_loop(0, bands, term, 0)

        def send(d, carry):
            g = lax.rem(f + d, freqs)
            pltpu.make_async_remote_copy(
                image_tx.at[z, pl.ds(pl.multiple_of(g * rows, rows), rows)],
                image_rx.at[z, f],
                image_send.at[z],
                image_recv.at[z],
                device_id={"freq": g},
                device_id_type=MESH,
            ).start()
            return carry

        lax.fori_loop(1, freqs, send, 0)
        pltpu.make_async_copy(
            image_tx.at[z, pl.ds(pl.multiple_of(f * rows, rows), rows)],
            image_rx.at[z, f],
            image_recv.at[z],
        ).start()

    def layer(z, carry):
        for u in range(2):

            @pl.when(z > 0)
            def _():
                to_fields(u)

            to_wavenumbers(z, u)

        @pl.when(z > 0)
        def _():
            send_image(z - 1)

        @pl.when(z == 0)
        def _():
            wait_bytes(slow.at[pl.ds(1, depth - 1)], slow_recv.at[1])
            for later in range(1, depth):
                make_trig(later)

        for u in range(2):
            turn(z, u)
        return carry

    lax.fori_loop(0, depth, layer, 0)
    for u in range(2):
        to_fields(u)
    send_image(depth - 1)
    for u in range(2):
        for c in range(2):
            bottom[0, 2 * u + c] = fields[u, :, c * strip : (c + 1) * strip]

    for z in range(depth):
        wait_bytes(image_rx.at[z], image_recv.at[z])
        image[z] = jnp.sum(image_rx[z].astype(F32), axis=0)

    wait_bytes(chunk_tx.at[pl.ds(0, freqs - 1)], chunk_send)
    wait_bytes(slow.at[0, pl.ds(0, freqs - 1)], slow_send.at[0])
    wait_bytes(slow.at[pl.ds(1, depth - 1), pl.ds(0, freqs - 1)], slow_send.at[1])
    for u in range(2):
        wait_bytes(tx.at[u, :, pl.ds(0, lateral - strip)], fwd_send.at[u])
        wait_bytes(ptx.at[u, pl.ds(0, bands - 1)], back_send.at[u])
    for z in range(depth):
        wait_bytes(image_tx.at[z, pl.ds(0, lateral - rows)], image_send.at[z])


def body(wavefields, slowness_store, owner_plan, freq_slot):
    freqs = lax.axis_size("freq")
    bands = lax.axis_size("band")
    lateral = wavefields.shape[2]
    depth = owner_plan.shape[0]
    strip = lateral // bands
    rows = lateral // freqs
    dims = (freqs, bands, lateral, depth)
    smem = pl.BlockSpec(memory_space=pltpu.SMEM)
    vmem = pl.BlockSpec(memory_space=pltpu.VMEM)
    dma = pltpu.SemaphoreType.DMA
    return pl.pallas_call(
        functools.partial(kernel, dims),
        out_shape=(
            jax.ShapeDtypeStruct((depth, rows, strip), F32),
            jax.ShapeDtypeStruct((1, 4, lateral, strip), F32),
        ),
        in_specs=[smem, smem, vmem, vmem, pl.BlockSpec(memory_space=pl.ANY)],
        out_specs=(vmem, vmem),
        scratch_shapes=[
            pltpu.VMEM((2, lateral, 2 * strip), F32),
            pltpu.VMEM((2, lateral, 2 * strip), BF16),
            pltpu.VMEM((2, 2, lateral, strip), BF16),
            pltpu.VMEM((2, 2, strip, lateral), BF16),
            pltpu.VMEM((2, 2 * strip, lateral), BF16),
            pltpu.VMEM((2, bands, strip, 2 * strip), BF16),
            pltpu.VMEM((2, lateral, 2 * strip), BF16),
            pltpu.VMEM((depth, 2, lateral, strip), F32),
            pltpu.VMEM((2, strip, lateral), F32),
            pltpu.VMEM((freqs, rows + 16, strip), BF16),
            pltpu.VMEM((freqs, rows + 16, strip), BF16),
            pltpu.VMEM((depth, rows, strip), BF16),
            pltpu.VMEM((depth, freqs, rows, strip), BF16),
            pltpu.VMEM((depth, lateral, strip), BF16),
            pltpu.VMEM((depth, freqs, rows, strip), BF16),
            dma,
            dma,
            dma,
            dma((2,)),
            dma((2,)),
            dma((2,)),
            dma((2,)),
            dma((2,)),
            dma((2,)),
            dma((depth,)),
            dma((depth,)),
        ],
        compiler_params=pltpu.CompilerParams(
            collective_id=0, has_side_effects=True, vmem_limit_bytes=48 * 2**20
        ),
    )(owner_plan, freq_slot, jnp.asarray(sine_table(lateral)), slowness_store, wavefields)


def solution(mesh):
    in_specs = (P("freq", None, None, "band"), P("freq", None, "band"), P(), P("freq"))
    out_specs = (P(None, "freq", "band"), P("freq", None, None, "band"))
    return jax.shard_map(body, mesh=mesh, in_specs=in_specs, out_specs=out_specs, check_vma=False)
```

```python
import functools
import math

import jax
import jax.numpy as jnp
import numpy as np
from jax import lax
from jax.experimental import pallas as pl
from jax.experimental.pallas import tpu as pltpu
from jax.sharding import PartitionSpec as P

OMEGA_LO = 1.5
OMEGA_HI = 3.0
MESH = pl.DeviceIdType.MESH
BF16 = jnp.bfloat16
F32 = jnp.float32


def sine_table(length):
    ordinal = np.arange(1, length + 1, dtype=np.int64)
    modulo = ordinal[:, None] * ordinal[None, :] % (2 * (length + 1))
    angles = math.pi * modulo / (length + 1)
    return (math.sqrt(2.0 / (length + 1)) * np.sin(angles)).astype(np.float32).astype(BF16)


def small_cos_sin(phi):
    p2 = phi * phi
    cosine = 1.0 + p2 * (-1 / 2 + p2 * (1 / 24 + p2 * (-1 / 720 + p2 * (1 / 40320))))
    sine = phi * (1.0 + p2 * (-1 / 6 + p2 * (1 / 120 + p2 * (-1 / 5040 + p2 * (1 / 362880)))))
    return cosine, sine


def kernel(
    dims,
    owner,
    slot,
    table,
    slab,
    wave,
    image,
    bottom,
    fields,
    shifted,
    tx,
    mid,
    rx,
    turned,
    ptx,
    prx,
    last,
    trig,
    factor,
    chunk_tx,
    chunk_rx,
    select,
    slow,
    column,
    slow_mid,
    cross_tx,
    cross_rx,
    plane_tx,
    plane_rx,
    column_tx,
    column_rx,
    image_tx,
    image_rx,
    load_sem,
    chunk_send,
    chunk_recv,
    slow_send,
    slow_recv,
    column_send,
    column_recv,
    slow_mid_send,
    slow_mid_recv,
    fwd_send,
    fwd_recv,
    mid_send,
    mid_recv,
    back_send,
    back_recv,
    last_send,
    last_recv,
    cross_send,
    cross_recv,
    plane_send,
    plane_recv,
    up_send,
    up_recv,
    image_send,
    image_recv,
):
    freqs, bands, lateral, depth = dims
    n = bands // 2
    strip = lateral // bands
    rows = lateral // freqs
    tile = 2 * strip
    f = lax.axis_index("freq")
    b = lax.axis_index("band")
    x, y, l = lax.rem(f, n), lax.rem(f // n, n), f // (n * n)
    h, c = b // 2, lax.rem(b, 2)
    z = 2 * h + l
    ring = (x, y)
    other = (y, x)
    home = tuple(lax.rem(h - other[u] + n, n) for u in range(2))
    numbers = (l * n * n + y * n + home[0], l * n * n + home[1] * n + x)
    strips = tuple(2 * ring[u] + c for u in range(2))

    def at(u, r, o, zz, cc):
        xx, yy = (r, o) if u == 0 else (o, r)
        return {"freq": (lax.rem(zz, 2) * n + yy) * n + xx, "band": (zz // 2) * 2 + cc}

    def wait_bytes(ref, sem):
        pltpu.make_async_copy(ref, ref, sem).wait()

    def remote(src, dst, send_sem, recv_sem, target):
        pltpu.make_async_remote_copy(
            src, dst, send_sem, recv_sem, device_id=target, device_id_type=MESH
        ).start()

    def send(src, dst, send_sem, recv_sem, target, here):
        @pl.when(jnp.logical_not(here))
        def _():
            remote(src, dst, send_sem, recv_sem, target)

        @pl.when(here)
        def _():
            pltpu.make_async_copy(src, dst, recv_sem).start()

    def loop(first, count, body):
        def step(i, carry):
            body(i)
            return carry

        lax.fori_loop(first, count, step, 0)

    def aligned(i, size):
        return pl.ds(pl.multiple_of(i * size, size), size)

    barrier = pltpu.get_barrier_semaphore()

    def greet(axis, me, count):
        def body(d):
            pl.semaphore_signal(
                barrier, inc=1, device_id={axis: lax.rem(me + d, count)}, device_id_type=MESH
            )

        loop(1, count, body)

    greet("freq", f, freqs)
    greet("band", b, bands)
    loads = [
        pltpu.make_async_copy(
            wave.at[0, 2 * u + k], fields.at[u, :, pl.ds(k * strip, strip)], load_sem
        )
        for u in range(2)
        for k in range(2)
    ]
    for load in loads:
        load.start()
    chunk_tx[:, 0:rows, :] = (slab[0] - 1.0).astype(BF16).reshape(freqs, rows, strip)
    chunk_tx[:, rows:, :] = jnp.full((freqs, 16, strip), slot[0].astype(F32)).astype(BF16)
    pl.semaphore_wait(barrier, freqs + bands - 2)

    def send_chunk(d):
        g = lax.rem(f + d, freqs)
        remote(chunk_tx.at[g], chunk_rx.at[f], chunk_send, chunk_recv, {"freq": g})

    loop(1, freqs, send_chunk)
    pltpu.make_async_copy(chunk_tx.at[f], chunk_rx.at[f], chunk_recv).start()

    def omega_of(number):
        return OMEGA_LO + (OMEGA_HI - OMEGA_LO) * (number.astype(F32) + 0.5) / freqs

    omega = omega_of(slot[0])

    wait_bytes(chunk_rx, chunk_recv)
    for k in range(depth):
        select[k] = chunk_rx[owner[k], 0:rows, :]

    def send_slow(d):
        g = lax.rem(f + d, freqs)
        remote(select.at[0], slow.at[f], slow_send, slow_recv, {"freq": g})

    loop(1, freqs, send_slow)
    pltpu.make_async_copy(select.at[0], slow.at[f], slow_recv).start()

    def send_column(d):
        zz = lax.rem(z + d, bands)
        remote(
            select.at[pl.ds(1, depth - 1)],
            column.at[z],
            column_send,
            column_recv,
            at(0, x, y, zz, c),
        )

    loop(1, bands, send_column)
    pltpu.make_async_copy(select.at[pl.ds(1, depth - 1)], column.at[z], column_recv).start()

    def send_planes():
        wait_bytes(column, column_recv)
        for u in range(2):

            def body(i, u=u):
                hh, oo = i // n, lax.rem(i, n)
                send(
                    column.at[pl.ds(2 * hh, 2)],
                    slow_mid.at[u, :, y * n + x],
                    slow_mid_send.at[u],
                    slow_mid_recv.at[u],
                    at(u, hh, oo, z, c),
                    (hh == ring[u]) & (oo == other[u]),
                )

            loop(0, n * n, body)

    def make_factor(u):
        mine = omega_of(chunk_rx[numbers[u], rows : rows + 16, :])[0:1]

        def body(i):
            shape = (strip, strip)
            kx = (lax.broadcasted_iota(jnp.int32, shape, 0) + (strips[u] * strip + 1)).astype(F32)
            ky = (lax.broadcasted_iota(jnp.int32, shape, 1) + (i * strip + 1)).astype(F32)
            kx = math.pi * kx / (lateral + 1)
            ky = math.pi * ky / (lateral + 1)
            q = mine * mine - kx * kx - ky * ky
            theta = jnp.sqrt(jnp.maximum(q, 0.0))
            damp = jnp.exp(-jnp.sqrt(jnp.maximum(-q, 0.0)))
            factor[u, 0, :, aligned(i, strip)] = damp * jnp.cos(theta)
            factor[u, 1, :, aligned(i, strip)] = damp * jnp.sin(theta)

        loop(0, bands, body)

    def make_first_trig():
        def body(g):
            cosine, sine = small_cos_sin(omega * slow[g].astype(F32))
            trig[0, 0, aligned(g, rows)] = cosine
            trig[0, 1, aligned(g, rows)] = sine

        loop(0, freqs, body)

    def make_trig(step, u):
        mine = omega_of(chunk_rx[numbers[u], rows : rows + 16, :])[0:1]

        def body(g):
            value = slow_mid[u, g // (n * n), lax.rem(g, n * n), step - 1]
            cosine, sine = small_cos_sin(mine * value.astype(F32))
            trig[2 * step - 1 + u, 0, aligned(g, rows)] = cosine
            trig[2 * step - 1 + u, 1, aligned(g, rows)] = sine

        loop(0, freqs, body)

    def hand(u):
        return -1.0 if u == 0 else 1.0

    def to_wavenumbers(step, u):
        phase = 0 if step == 0 else 2 * step - 1 + u

        def shift(i):
            block = aligned(i, strip)
            cosine = trig[phase, 0, block]
            sine = trig[phase, 1, block] * hand(u)
            re = fields[u, block, 0:strip]
            im = fields[u, block, strip:]
            shifted[u, block, 0:strip] = (re * cosine - im * sine).astype(BF16)
            shifted[u, block, strip:] = (im * cosine + re * sine).astype(BF16)

        loop(0, bands, shift)
        if step > 0:
            wait_bytes(tx.at[u, :, pl.ds(0, lateral - strip)], fwd_send.at[u])

        def product(i):
            t = lax.rem(ring[u] + 1 + i, n)
            block = aligned(t, tile)
            half = jnp.dot(table[block, :], shifted[u], preferred_element_type=F32).astype(BF16)
            tx[u, 0, block] = half[:, 0:strip]
            tx[u, 1, block] = half[:, strip:]
            for p in range(2):
                j = 2 * t + p
                if step == 0:
                    dst = mid.at[u, ring[u], :, :, aligned(c, strip)]
                    sem = mid_recv.at[u, ring[u]]
                else:
                    dst = rx.at[u, :, :, aligned(strips[u], strip)]
                    sem = fwd_recv.at[u]
                send(
                    tx.at[u, :, aligned(j, strip)],
                    dst,
                    fwd_send.at[u],
                    sem,
                    at(u, t, other[u], z, p),
                    j == strips[u],
                )

        loop(0, n, product)

    def forward(u):
        def body(i):
            q = lax.rem(ring[u] + i, n)
            wait_bytes(mid.at[u, q], mid_recv.at[u, q])
            hh = lax.rem(q + other[u], n)
            send(
                mid.at[u, q],
                rx.at[u, :, :, aligned(h, tile)],
                mid_send.at[u],
                fwd_recv.at[u],
                at(u, ring[u], other[u], 2 * hh + l, c),
                hh == h,
            )

        loop(0, n, body)

    def turn(step, u):
        wait_bytes(rx.at[u], fwd_recv.at[u])

        def product(i):
            lanes = aligned(i, tile)
            lines = rx[u].reshape(2 * strip, lateral)
            spectrum = jnp.dot(lines, table[:, lanes], preferred_element_type=F32)
            re = spectrum[0:strip]
            im = spectrum[strip:]
            cosine = factor[u, 0, :, lanes]
            sine = factor[u, 1, :, lanes] * hand(u)
            turned[u, 0:strip, lanes] = (re * cosine - im * sine).astype(BF16)
            turned[u, strip:, lanes] = (im * cosine + re * sine).astype(BF16)

        loop(0, n, product)
        if step > 0:
            wait_bytes(ptx.at[u, pl.ds(0, bands - 1)], back_send.at[u])
        final = step == depth - 1

        def back(i):
            t = lax.rem((h if final else ring[u]) + 1 + i, n)
            lanes = aligned(t, tile)
            partial = jnp.dot(turned[u], table[:, lanes], preferred_element_type=F32).astype(BF16)
            for p in range(2):
                j = 2 * t + p
                cols = slice(p * strip, (p + 1) * strip)
                ptx[u, j, :, 0:strip] = partial[0:strip, cols]
                ptx[u, j, :, strip:] = partial[strip:, cols]
                block = aligned(strips[u], strip)
                if final:
                    send(
                        ptx.at[u, j],
                        last.at[u, block],
                        last_send.at[u],
                        last_recv.at[u],
                        at(u, home[u], other[u], 2 * t + l, p),
                        (home[u] == ring[u]) & (j == b),
                    )
                else:
                    send(
                        ptx.at[u, j],
                        prx.at[u, block],
                        back_send.at[u],
                        back_recv.at[u],
                        at(u, t, other[u], z, p),
                        j == strips[u],
                    )

        loop(0, n, back)

    def to_fields(u, source, sem):
        wait_bytes(source.at[u], sem.at[u])

        def product(i):
            block = aligned(i, tile)
            fields[u, block] = jnp.dot(table[block, :], source[u], preferred_element_type=F32)

        loop(0, n, product)

    normalizer = 1.0 / math.sqrt(freqs)

    def send_cross(step):
        def body(i):
            cross_tx[step, aligned(i, strip)] = fields[1, aligned(i, strip)].astype(BF16)

        loop(0, bands, body)
        send(
            cross_tx.at[step],
            cross_rx.at[step],
            cross_send.at[step],
            cross_recv.at[step],
            at(0, y, home[1], z, c),
            (x == y) & (home[1] == y),
        )

    def send_terms(step):
        wait_bytes(cross_rx.at[step], cross_recv.at[step])

        def body(g):
            block = aligned(g, rows)
            value = fields[0, block] * cross_rx[step, block].astype(F32)
            value = (value[:, 0:strip] + value[:, strip:]) * normalizer
            plane_tx[step, g // (n * n), lax.rem(g, n * n)] = value.astype(BF16)

        loop(0, freqs, body)

        def body_send(i):
            g = lax.rem(y * n + x + i, n * n)
            send(
                plane_tx.at[step, :, g],
                plane_rx.at[step, x, y],
                plane_send.at[step],
                plane_recv.at[step],
                at(0, lax.rem(g, n), g // n, z, c),
                i == 0,
            )

        loop(0, n * n, body_send)

    def send_sums(step):
        wait_bytes(plane_rx.at[step], plane_recv.at[step])

        def body(i):
            zz = lax.rem(z + i, bands)
            total = jnp.zeros((rows, strip), F32)
            for yy in range(n):
                total += plane_rx[step, zz // 2, yy, lax.rem(zz, 2)].astype(F32)
            column_tx[step, zz] = total.astype(BF16)
            send(
                column_tx.at[step, zz],
                column_rx.at[step, z],
                up_send.at[step],
                up_recv.at[step],
                at(0, x, y, zz, c),
                i == 0,
            )

        loop(0, bands, body)

    def send_image():
        def term(i):
            block = aligned(i, strip)
            value = fields[0, block] * fields[1, block]
            value = (value[:, 0:strip] + value[:, strip:]) * normalizer
            image_tx[block] = value.astype(BF16)

        loop(0, bands, term)

        def body(d):
            g = lax.rem(f + d, freqs)
            remote(
                image_tx.at[aligned(g, rows)], image_rx.at[f], image_send, image_recv, {"freq": g}
            )

        loop(1, freqs, body)
        pltpu.make_async_copy(image_tx.at[aligned(f, rows)], image_rx.at[f], image_recv).start()

    for load in loads:
        load.wait()
    wait_bytes(slow, slow_recv)
    make_first_trig()
    for step in range(depth):
        for u in range(2):
            if step > 0:
                to_fields(u, prx, back_recv)
            to_wavenumbers(step, u)
        if step == 0:
            for u in range(2):
                forward(u)
            send_planes()
            for u in range(2):
                make_factor(u)
        else:
            send_cross(step - 1)
        for u in range(2):
            turn(step, u)
        if step > 0:
            send_terms(step - 1)
        if step == 0:
            for u in range(2):
                wait_bytes(slow_mid.at[u], slow_mid_recv.at[u])
        if step < depth - 1:
            for u in range(2):
                make_trig(step + 1, u)
        if step > 1:
            send_sums(step - 2)
    send_sums(depth - 2)
    for u in range(2):
        to_fields(u, last, last_recv)
    send_image()
    for u in range(2):
        for k in range(2):
            bottom[0, 2 * u + k] = fields[u, :, k * strip : (k + 1) * strip]

    for step in range(depth - 1):
        wait_bytes(column_rx.at[step], up_recv.at[step])
        image[step] = jnp.sum(column_rx[step].astype(F32), axis=0)
    wait_bytes(image_rx, image_recv)
    image[depth - 1] = jnp.sum(image_rx[...].astype(F32), axis=0)

    wait_bytes(chunk_tx.at[pl.ds(0, freqs - 1)], chunk_send)
    wait_bytes(slow.at[pl.ds(0, freqs - 1)], slow_send)
    wait_bytes(column.at[pl.ds(0, bands - 1)], column_send)
    for u in range(2):
        wait_bytes(slow_mid.at[u, :, pl.ds(0, n * n - 1)], slow_mid_send.at[u])
        wait_bytes(mid.at[u, pl.ds(0, n - 1)], mid_send.at[u])
        wait_bytes(tx.at[u, :, pl.ds(0, lateral - strip)], fwd_send.at[u])
        wait_bytes(ptx.at[u, pl.ds(0, bands - 1)], last_send.at[u])

        @pl.when(home[u] != ring[u])
        def _():
            wait_bytes(ptx.at[u, 0], last_send.at[u])

    for step in range(depth - 1):

        @pl.when(jnp.logical_not((x == y) & (home[1] == y)))
        def _():
            wait_bytes(cross_tx.at[step], cross_send.at[step])

        wait_bytes(plane_tx.at[step, :, pl.ds(0, n * n - 1)], plane_send.at[step])
        wait_bytes(column_tx.at[step, pl.ds(0, bands - 1)], up_send.at[step])
    wait_bytes(image_tx.at[pl.ds(0, lateral - rows)], image_send)


def body(wavefields, slowness_store, owner_plan, freq_slot):
    freqs = lax.axis_size("freq")
    bands = lax.axis_size("band")
    lateral = wavefields.shape[2]
    depth = owner_plan.shape[0]
    n = bands // 2
    strip = lateral // bands
    rows = lateral // freqs
    dims = (freqs, bands, lateral, depth)
    smem = pl.BlockSpec(memory_space=pltpu.SMEM)
    vmem = pl.BlockSpec(memory_space=pltpu.VMEM)
    dma = pltpu.SemaphoreType.DMA
    return pl.pallas_call(
        functools.partial(kernel, dims),
        out_shape=(
            jax.ShapeDtypeStruct((depth, rows, strip), F32),
            jax.ShapeDtypeStruct((1, 4, lateral, strip), F32),
        ),
        in_specs=[smem, smem, vmem, vmem, pl.BlockSpec(memory_space=pl.ANY)],
        out_specs=(vmem, vmem),
        scratch_shapes=[
            pltpu.VMEM((2, lateral, 2 * strip), F32),
            pltpu.VMEM((2, lateral, 2 * strip), BF16),
            pltpu.VMEM((2, 2, lateral, strip), BF16),
            pltpu.VMEM((2, n, 2, strip, 2 * strip), BF16),
            pltpu.VMEM((2, 2, strip, lateral), BF16),
            pltpu.VMEM((2, 2 * strip, lateral), BF16),
            pltpu.VMEM((2, bands, strip, 2 * strip), BF16),
            pltpu.VMEM((2, lateral, 2 * strip), BF16),
            pltpu.VMEM((2, lateral, 2 * strip), BF16),
            pltpu.VMEM((2 * depth - 1, 2, lateral, strip), F32),
            pltpu.VMEM((2, 2, strip, lateral), F32),
            pltpu.VMEM((freqs, rows + 16, strip), BF16),
            pltpu.VMEM((freqs, rows + 16, strip), BF16),
            pltpu.VMEM((depth, rows, strip), BF16),
            pltpu.VMEM((freqs, rows, strip), BF16),
            pltpu.VMEM((bands, depth - 1, rows, strip), BF16),
            pltpu.VMEM((2, 2, n * n, depth - 1, rows, strip), BF16),
            pltpu.VMEM((depth - 1, lateral, 2 * strip), BF16),
            pltpu.VMEM((depth - 1, lateral, 2 * strip), BF16),
            pltpu.VMEM((depth - 1, 2, n * n, rows, strip), BF16),
            pltpu.VMEM((depth - 1, n, n, 2, rows, strip), BF16),
            pltpu.VMEM((depth - 1, bands, rows, strip), BF16),
            pltpu.VMEM((depth - 1, bands, rows, strip), BF16),
            pltpu.VMEM((lateral, strip), BF16),
            pltpu.VMEM((freqs, rows, strip), BF16),
            dma,
            dma,
            dma,
            dma,
            dma,
            dma,
            dma,
            dma((2,)),
            dma((2,)),
            dma((2,)),
            dma((2,)),
            dma((2,)),
            dma((2, n)),
            dma((2,)),
            dma((2,)),
            dma((2,)),
            dma((2,)),
            dma((depth - 1,)),
            dma((depth - 1,)),
            dma((depth - 1,)),
            dma((depth - 1,)),
            dma((depth - 1,)),
            dma((depth - 1,)),
            dma,
            dma,
        ],
        compiler_params=pltpu.CompilerParams(
            collective_id=0, has_side_effects=True, vmem_limit_bytes=52 * 2**20
        ),
    )(owner_plan, freq_slot, jnp.asarray(sine_table(lateral)), slowness_store, wavefields)


def solution(mesh):
    in_specs = (P("freq", None, None, "band"), P("freq", None, "band"), P(), P("freq"))
    out_specs = (P(None, "freq", "band"), P("freq", None, None, "band"))
    return jax.shard_map(body, mesh=mesh, in_specs=in_specs, out_specs=out_specs, check_vma=False)
```

```python
import functools
import math

import jax
import jax.numpy as jnp
import numpy as np
from jax import lax
from jax.experimental import pallas as pl
from jax.experimental.pallas import tpu as pltpu
from jax.sharding import PartitionSpec as P

OMEGA_LO = 1.5
OMEGA_HI = 3.0
MESH = pl.DeviceIdType.MESH
BF16 = jnp.bfloat16
F32 = jnp.float32


def sine_table(length):
    ordinal = np.arange(1, length + 1, dtype=np.int64)
    modulo = ordinal[:, None] * ordinal[None, :] % (2 * (length + 1))
    angles = math.pi * modulo / (length + 1)
    return (math.sqrt(2.0 / (length + 1)) * np.sin(angles)).astype(np.float32).astype(BF16)


def small_cos_sin(phi):
    p2 = phi * phi
    cosine = 1.0 + p2 * (-1 / 2 + p2 * (1 / 24 + p2 * (-1 / 720 + p2 * (1 / 40320))))
    sine = phi * (1.0 + p2 * (-1 / 6 + p2 * (1 / 120 + p2 * (-1 / 5040 + p2 * (1 / 362880)))))
    return cosine, sine


def kernel(
    dims,
    owner,
    slot,
    table,
    slab,
    wave,
    image,
    bottom,
    fields,
    shifted,
    tx,
    mid,
    rx,
    turned,
    ptx,
    prx,
    last,
    trig,
    factor,
    chunk_tx,
    chunk_rx,
    select,
    slow,
    column,
    slow_mid,
    keep,
    cross_tx,
    cross_rx,
    plane_tx,
    plane_rx,
    column_tx,
    column_rx,
    image_tx,
    image_rx,
    load_sem,
    chunk_send,
    chunk_recv,
    slow_send,
    slow_recv,
    column_send,
    column_recv,
    slow_mid_send,
    slow_mid_recv,
    fwd_send,
    fwd_recv,
    mid_send,
    mid_recv,
    back_send,
    back_recv,
    last_send,
    last_recv,
    cross_send,
    cross_recv,
    plane_send,
    plane_recv,
    up_send,
    up_recv,
    image_send,
    image_recv,
):
    freqs, bands, lateral, depth = dims
    n = bands // 2
    strip = lateral // bands
    rows = lateral // freqs
    tile = 2 * strip
    f = lax.axis_index("freq")
    b = lax.axis_index("band")
    x, y, l = lax.rem(f, n), lax.rem(f // n, n), f // (n * n)
    h, c = b // 2, lax.rem(b, 2)
    z = 2 * h + l
    ring = (x, y)
    other = (y, x)
    home = tuple(lax.rem(h - other[u] + n, n) for u in range(2))
    numbers = (l * n * n + y * n + home[0], l * n * n + home[1] * n + x)
    place = (x, lax.rem(y - x + n, n))
    strips = tuple(2 * place[u] + c for u in range(2))

    def spot(u, t, o):
        return t if u == 0 else lax.rem(t + o, n)

    def at(u, r, o, zz, cc):
        xx, yy = (r, o) if u == 0 else (o, r)
        return {"freq": (lax.rem(zz, 2) * n + yy) * n + xx, "band": (zz // 2) * 2 + cc}

    def wait_bytes(ref, sem):
        pltpu.make_async_copy(ref, ref, sem).wait()

    def remote(src, dst, send_sem, recv_sem, target):
        pltpu.make_async_remote_copy(
            src, dst, send_sem, recv_sem, device_id=target, device_id_type=MESH
        ).start()

    def send(src, dst, send_sem, recv_sem, target, here):
        @pl.when(jnp.logical_not(here))
        def _():
            remote(src, dst, send_sem, recv_sem, target)

        @pl.when(here)
        def _():
            pltpu.make_async_copy(src, dst, recv_sem).start()

    def loop(first, count, body):
        def step(i, carry):
            body(i)
            return carry

        lax.fori_loop(first, count, step, 0)

    def aligned(i, size):
        return pl.ds(pl.multiple_of(i * size, size), size)

    barrier = pltpu.get_barrier_semaphore()

    def greet(axis, me, count):
        def body(d):
            pl.semaphore_signal(
                barrier, inc=1, device_id={axis: lax.rem(me + d, count)}, device_id_type=MESH
            )

        loop(1, count, body)

    greet("freq", f, freqs)
    greet("band", b, bands)
    loads = [
        pltpu.make_async_copy(
            wave.at[0, 2 * u + k], fields.at[u, :, pl.ds(k * strip, strip)], load_sem
        )
        for u in range(2)
        for k in range(2)
    ]
    for load in loads:
        load.start()
    chunk_tx[:, 0:rows, :] = (slab[0] - 1.0).astype(BF16).reshape(freqs, rows, strip)
    chunk_tx[:, rows:, :] = jnp.full((freqs, 16, strip), slot[0].astype(F32)).astype(BF16)
    pl.semaphore_wait(barrier, freqs + bands - 2)

    def send_chunk(d):
        g = lax.rem(f + d, freqs)
        remote(chunk_tx.at[g], chunk_rx.at[f], chunk_send, chunk_recv, {"freq": g})

    loop(1, freqs, send_chunk)
    pltpu.make_async_copy(chunk_tx.at[f], chunk_rx.at[f], chunk_recv).start()

    def omega_of(number):
        return OMEGA_LO + (OMEGA_HI - OMEGA_LO) * (number.astype(F32) + 0.5) / freqs

    omega = omega_of(slot[0])

    wait_bytes(chunk_rx, chunk_recv)
    for k in range(depth):
        select[k] = chunk_rx[owner[k], 0:rows, :]

    def send_slow(d):
        g = lax.rem(f + d, freqs)
        remote(select.at[0], slow.at[f], slow_send, slow_recv, {"freq": g})

    loop(1, freqs, send_slow)
    pltpu.make_async_copy(select.at[0], slow.at[f], slow_recv).start()

    def send_column(d):
        zz = lax.rem(z + d, bands)
        remote(
            select.at[pl.ds(1, depth - 1)],
            column.at[z],
            column_send,
            column_recv,
            at(0, x, y, zz, c),
        )

    loop(1, bands, send_column)
    pltpu.make_async_copy(select.at[pl.ds(1, depth - 1)], column.at[z], column_recv).start()

    def send_planes():
        wait_bytes(column, column_recv)
        for u in range(2):

            def body(i, u=u):
                hh, oo = i // n, lax.rem(i, n)
                send(
                    column.at[pl.ds(2 * hh, 2)],
                    slow_mid.at[u, :, y * n + x],
                    slow_mid_send.at[u],
                    slow_mid_recv.at[u],
                    at(u, spot(u, hh, oo), oo, z, c),
                    (hh == place[u]) & (oo == other[u]),
                )

            loop(0, n * n, body)

    def make_factor(u):
        mine = omega_of(chunk_rx[numbers[u], rows : rows + 16, :])[0:1]

        def body(i):
            shape = (strip, strip)
            kx = (lax.broadcasted_iota(jnp.int32, shape, 0) + (strips[u] * strip + 1)).astype(F32)
            ky = (lax.broadcasted_iota(jnp.int32, shape, 1) + (i * strip + 1)).astype(F32)
            kx = math.pi * kx / (lateral + 1)
            ky = math.pi * ky / (lateral + 1)
            q = mine * mine - kx * kx - ky * ky
            theta = jnp.sqrt(jnp.maximum(q, 0.0))
            damp = jnp.exp(-jnp.sqrt(jnp.maximum(-q, 0.0)))
            factor[u, 0, :, aligned(i, strip)] = damp * jnp.cos(theta)
            factor[u, 1, :, aligned(i, strip)] = damp * jnp.sin(theta)

        loop(0, bands, body)

    def make_first_trig():
        def body(g):
            cosine, sine = small_cos_sin(omega * slow[g].astype(F32))
            trig[0, 0, aligned(g, rows)] = cosine
            trig[0, 1, aligned(g, rows)] = sine

        loop(0, freqs, body)

    def make_trig(step, u):
        mine = omega_of(chunk_rx[numbers[u], rows : rows + 16, :])[0:1]

        def body(g):
            value = slow_mid[u, g // (n * n), lax.rem(g, n * n), step - 1]
            cosine, sine = small_cos_sin(mine * value.astype(F32))
            trig[2 * step - 1 + u, 0, aligned(g, rows)] = cosine
            trig[2 * step - 1 + u, 1, aligned(g, rows)] = sine

        loop(0, freqs, body)

    def hand(u):
        return -1.0 if u == 0 else 1.0

    def to_wavenumbers(step, u):
        phase = 0 if step == 0 else 2 * step - 1 + u

        def shift(i):
            block = aligned(i, strip)
            cosine = trig[phase, 0, block]
            sine = trig[phase, 1, block] * hand(u)
            re = fields[u, block, 0:strip]
            im = fields[u, block, strip:]
            shifted[u, block, 0:strip] = (re * cosine - im * sine).astype(BF16)
            shifted[u, block, strip:] = (im * cosine + re * sine).astype(BF16)

        loop(0, bands, shift)
        if step > 0:
            wait_bytes(tx.at[u, :, pl.ds(0, lateral - strip)], fwd_send.at[u])

        def product(i):
            t = lax.rem(place[u] + 1 + i, n)
            block = aligned(t, tile)
            half = jnp.dot(table[block, :], shifted[u], preferred_element_type=F32).astype(BF16)
            tx[u, 0, block] = half[:, 0:strip]
            tx[u, 1, block] = half[:, strip:]
            for p in range(2):
                j = 2 * t + p
                if step == 0:
                    dst = mid.at[u, ring[u], :, :, aligned(c, strip)]
                    sem = mid_recv.at[u, ring[u]]
                else:
                    dst = rx.at[u, :, :, aligned(strips[u], strip)]
                    sem = fwd_recv.at[u]
                send(
                    tx.at[u, :, aligned(j, strip)],
                    dst,
                    fwd_send.at[u],
                    sem,
                    at(u, spot(u, t, other[u]), other[u], z, p),
                    j == strips[u],
                )

        loop(0, n, product)

    def forward(u):
        def body(i):
            q = lax.rem(ring[u] + i, n)
            wait_bytes(mid.at[u, q], mid_recv.at[u, q])
            hh = lax.rem(q + other[u], n)
            send(
                mid.at[u, q],
                rx.at[u, :, :, aligned(h, tile)],
                mid_send.at[u],
                fwd_recv.at[u],
                at(u, ring[u], other[u], 2 * hh + l, c),
                hh == h,
            )

        loop(0, n, body)

    def turn(step, u):
        wait_bytes(rx.at[u], fwd_recv.at[u])

        def product(i):
            lanes = aligned(i, tile)
            lines = rx[u].reshape(2 * strip, lateral)
            spectrum = jnp.dot(lines, table[:, lanes], preferred_element_type=F32)
            re = spectrum[0:strip]
            im = spectrum[strip:]
            cosine = factor[u, 0, :, lanes]
            sine = factor[u, 1, :, lanes] * hand(u)
            turned[u, 0:strip, lanes] = (re * cosine - im * sine).astype(BF16)
            turned[u, strip:, lanes] = (im * cosine + re * sine).astype(BF16)

        loop(0, n, product)
        if step > 0:
            wait_bytes(ptx.at[u, pl.ds(0, bands - 1)], back_send.at[u])
        final = step == depth - 1

        def back(i):
            t = lax.rem((h if final else place[u]) + 1 + i, n)
            lanes = aligned(t, tile)
            partial = jnp.dot(turned[u], table[:, lanes], preferred_element_type=F32).astype(BF16)
            for p in range(2):
                j = 2 * t + p
                cols = slice(p * strip, (p + 1) * strip)
                ptx[u, j, :, 0:strip] = partial[0:strip, cols]
                ptx[u, j, :, strip:] = partial[strip:, cols]
                block = aligned(strips[u], strip)
                if final:
                    send(
                        ptx.at[u, j],
                        last.at[u, block],
                        last_send.at[u],
                        last_recv.at[u],
                        at(u, home[u], other[u], 2 * t + l, p),
                        (home[u] == ring[u]) & (j == b),
                    )
                else:
                    send(
                        ptx.at[u, j],
                        prx.at[u, block],
                        back_send.at[u],
                        back_recv.at[u],
                        at(u, spot(u, t, other[u]), other[u], z, p),
                        j == strips[u],
                    )

        loop(0, n, back)

    def to_fields(u, source, sem):
        wait_bytes(source.at[u], sem.at[u])

        def product(i):
            block = aligned(i, tile)
            fields[u, block] = jnp.dot(table[block, :], source[u], preferred_element_type=F32)

        loop(0, n, product)

    normalizer = 1.0 / math.sqrt(freqs)

    def keep_fields(step):
        def body(i):
            block = aligned(i, strip)
            keep[step, block] = fields[0, block].astype(BF16)
            cross_tx[step, block] = fields[1, block].astype(BF16)

        loop(0, bands, body)

    def send_cross(step):
        send(
            cross_tx.at[step],
            cross_rx.at[step],
            cross_send.at[step],
            cross_recv.at[step],
            at(0, place[1], home[1], z, c),
            (place[1] == x) & (home[1] == y),
        )

    def send_terms(step):
        wait_bytes(cross_rx.at[step], cross_recv.at[step])

        def body(g):
            block = aligned(g, rows)
            value = keep[step, block].astype(F32) * cross_rx[step, block].astype(F32)
            value = (value[:, 0:strip] + value[:, strip:]) * normalizer
            plane_tx[step, g // (n * n), lax.rem(g, n * n)] = value.astype(BF16)

        loop(0, freqs, body)

        def body_send(i):
            g = lax.rem(y * n + x + i, n * n)
            send(
                plane_tx.at[step, :, g],
                plane_rx.at[step, x, y],
                plane_send.at[step],
                plane_recv.at[step],
                at(0, lax.rem(g, n), g // n, z, c),
                i == 0,
            )

        loop(0, n * n, body_send)

    def send_sums(step):
        wait_bytes(plane_rx.at[step], plane_recv.at[step])

        def body(i):
            zz = lax.rem(z + i, bands)
            total = jnp.zeros((rows, strip), F32)
            for yy in range(n):
                total += plane_rx[step, zz // 2, yy, lax.rem(zz, 2)].astype(F32)
            column_tx[step, zz] = total.astype(BF16)
            send(
                column_tx.at[step, zz],
                column_rx.at[step, z],
                up_send.at[step],
                up_recv.at[step],
                at(0, x, y, zz, c),
                i == 0,
            )

        loop(0, bands, body)

    def send_image():
        def term(i):
            block = aligned(i, strip)
            value = fields[0, block] * fields[1, block]
            value = (value[:, 0:strip] + value[:, strip:]) * normalizer
            image_tx[block] = value.astype(BF16)

        loop(0, bands, term)

        def body(d):
            g = lax.rem(f + d, freqs)
            remote(
                image_tx.at[aligned(g, rows)], image_rx.at[f], image_send, image_recv, {"freq": g}
            )

        loop(1, freqs, body)
        pltpu.make_async_copy(image_tx.at[aligned(f, rows)], image_rx.at[f], image_recv).start()

    for u in range(2):
        make_factor(u)
    for load in loads:
        load.wait()
    wait_bytes(slow, slow_recv)
    make_first_trig()
    for step in range(depth):
        for u in range(2):
            if step > 0:
                to_fields(u, prx, back_recv)
            to_wavenumbers(step, u)
        if step == 0:
            for u in range(2):
                forward(u)
            send_planes()
        else:
            keep_fields(step - 1)
        for u in range(2):
            turn(step, u)
        if step > 0:
            send_cross(step - 1)
        if step == 0:
            for u in range(2):
                wait_bytes(slow_mid.at[u], slow_mid_recv.at[u])
        if step < depth - 1:
            for u in range(2):
                make_trig(step + 1, u)
    for step in range(depth - 1):
        send_terms(step)
    for step in range(depth - 2):
        send_sums(step)
    for u in range(2):
        to_fields(u, last, last_recv)
    send_image()
    send_sums(depth - 2)
    for u in range(2):
        for k in range(2):
            bottom[0, 2 * u + k] = fields[u, :, k * strip : (k + 1) * strip]

    for step in range(depth - 1):
        wait_bytes(column_rx.at[step], up_recv.at[step])
        image[step] = jnp.sum(column_rx[step].astype(F32), axis=0)
    wait_bytes(image_rx, image_recv)
    image[depth - 1] = jnp.sum(image_rx[...].astype(F32), axis=0)

    wait_bytes(chunk_tx.at[pl.ds(0, freqs - 1)], chunk_send)
    wait_bytes(slow.at[pl.ds(0, freqs - 1)], slow_send)
    wait_bytes(column.at[pl.ds(0, bands - 1)], column_send)
    for u in range(2):
        wait_bytes(slow_mid.at[u, :, pl.ds(0, n * n - 1)], slow_mid_send.at[u])
        wait_bytes(mid.at[u, pl.ds(0, n - 1)], mid_send.at[u])
        wait_bytes(tx.at[u, :, pl.ds(0, lateral - strip)], fwd_send.at[u])
        wait_bytes(ptx.at[u, pl.ds(0, bands - 1)], last_send.at[u])

        @pl.when(home[u] != ring[u])
        def _():
            wait_bytes(ptx.at[u, 0], last_send.at[u])

    for step in range(depth - 1):

        @pl.when(jnp.logical_not((place[1] == x) & (home[1] == y)))
        def _():
            wait_bytes(cross_tx.at[step], cross_send.at[step])

        wait_bytes(plane_tx.at[step, :, pl.ds(0, n * n - 1)], plane_send.at[step])
        wait_bytes(column_tx.at[step, pl.ds(0, bands - 1)], up_send.at[step])
    wait_bytes(image_tx.at[pl.ds(0, lateral - rows)], image_send)


def body(wavefields, slowness_store, owner_plan, freq_slot):
    freqs = lax.axis_size("freq")
    bands = lax.axis_size("band")
    lateral = wavefields.shape[2]
    depth = owner_plan.shape[0]
    n = bands // 2
    strip = lateral // bands
    rows = lateral // freqs
    dims = (freqs, bands, lateral, depth)
    smem = pl.BlockSpec(memory_space=pltpu.SMEM)
    vmem = pl.BlockSpec(memory_space=pltpu.VMEM)
    dma = pltpu.SemaphoreType.DMA
    return pl.pallas_call(
        functools.partial(kernel, dims),
        out_shape=(
            jax.ShapeDtypeStruct((depth, rows, strip), F32),
            jax.ShapeDtypeStruct((1, 4, lateral, strip), F32),
        ),
        in_specs=[smem, smem, vmem, vmem, pl.BlockSpec(memory_space=pl.ANY)],
        out_specs=(vmem, vmem),
        scratch_shapes=[
            pltpu.VMEM((2, lateral, 2 * strip), F32),
            pltpu.VMEM((2, lateral, 2 * strip), BF16),
            pltpu.VMEM((2, 2, lateral, strip), BF16),
            pltpu.VMEM((2, n, 2, strip, 2 * strip), BF16),
            pltpu.VMEM((2, 2, strip, lateral), BF16),
            pltpu.VMEM((2, 2 * strip, lateral), BF16),
            pltpu.VMEM((2, bands, strip, 2 * strip), BF16),
            pltpu.VMEM((2, lateral, 2 * strip), BF16),
            pltpu.VMEM((2, lateral, 2 * strip), BF16),
            pltpu.VMEM((2 * depth - 1, 2, lateral, strip), F32),
            pltpu.VMEM((2, 2, strip, lateral), F32),
            pltpu.VMEM((freqs, rows + 16, strip), BF16),
            pltpu.VMEM((freqs, rows + 16, strip), BF16),
            pltpu.VMEM((depth, rows, strip), BF16),
            pltpu.VMEM((freqs, rows, strip), BF16),
            pltpu.VMEM((bands, depth - 1, rows, strip), BF16),
            pltpu.VMEM((2, 2, n * n, depth - 1, rows, strip), BF16),
            pltpu.VMEM((depth - 1, lateral, 2 * strip), BF16),
            pltpu.VMEM((depth - 1, lateral, 2 * strip), BF16),
            pltpu.VMEM((depth - 1, lateral, 2 * strip), BF16),
            pltpu.VMEM((depth - 1, 2, n * n, rows, strip), BF16),
            pltpu.VMEM((depth - 1, n, n, 2, rows, strip), BF16),
            pltpu.VMEM((depth - 1, bands, rows, strip), BF16),
            pltpu.VMEM((depth - 1, bands, rows, strip), BF16),
            pltpu.VMEM((lateral, strip), BF16),
            pltpu.VMEM((freqs, rows, strip), BF16),
            dma,
            dma,
            dma,
            dma,
            dma,
            dma,
            dma,
            dma((2,)),
            dma((2,)),
            dma((2,)),
            dma((2,)),
            dma((2,)),
            dma((2, n)),
            dma((2,)),
            dma((2,)),
            dma((2,)),
            dma((2,)),
            dma((depth - 1,)),
            dma((depth - 1,)),
            dma((depth - 1,)),
            dma((depth - 1,)),
            dma((depth - 1,)),
            dma((depth - 1,)),
            dma,
            dma,
        ],
        compiler_params=pltpu.CompilerParams(
            collective_id=0, has_side_effects=True, vmem_limit_bytes=36 * 2**20
        ),
    )(owner_plan, freq_slot, jnp.asarray(sine_table(lateral)), slowness_store, wavefields)


def solution(mesh):
    in_specs = (P("freq", None, None, "band"), P("freq", None, "band"), P(), P("freq"))
    out_specs = (P(None, "freq", "band"), P("freq", None, None, "band"))
    return jax.shard_map(body, mesh=mesh, in_specs=in_specs, out_specs=out_specs, check_vma=False)
```

```python
import functools
import math

import jax
import jax.numpy as jnp
import numpy as np
from jax import lax
from jax.experimental import pallas as pl
from jax.experimental.pallas import tpu as pltpu
from jax.sharding import PartitionSpec as P

OMEGA_LO = 1.5
OMEGA_HI = 3.0
MESH = pl.DeviceIdType.MESH
BF16 = jnp.bfloat16
F32 = jnp.float32


def sine_table(length):
    ordinal = np.arange(1, length + 1, dtype=np.int64)
    modulo = ordinal[:, None] * ordinal[None, :] % (2 * (length + 1))
    angles = math.pi * modulo / (length + 1)
    return (math.sqrt(2.0 / (length + 1)) * np.sin(angles)).astype(np.float32).astype(BF16)


def small_cos_sin(phi):
    p2 = phi * phi
    cosine = 1.0 + p2 * (-1 / 2 + p2 * (1 / 24 + p2 * (-1 / 720 + p2 * (1 / 40320))))
    sine = phi * (1.0 + p2 * (-1 / 6 + p2 * (1 / 120 + p2 * (-1 / 5040 + p2 * (1 / 362880)))))
    return cosine, sine


def kernel(
    dims,
    owner,
    slot,
    table_hbm,
    slab_hbm,
    wave,
    image,
    bottom,
    table,
    slab,
    fields,
    shifted,
    tx,
    mid,
    rx,
    turned,
    ptx,
    prx,
    last,
    trig,
    factor,
    chunk_tx,
    chunk_rx,
    select,
    slow,
    column,
    slow_mid,
    kept,
    plane_tx,
    plane_rx,
    column_tx,
    column_rx,
    image_tx,
    image_rx,
    table_sem,
    slab_sem,
    load_sem,
    chunk_send,
    chunk_recv,
    slow_send,
    slow_recv,
    column_send,
    column_recv,
    slow_mid_send,
    slow_mid_recv,
    fwd_send,
    fwd_recv,
    mid_send,
    mid_recv,
    back_send,
    back_recv,
    last_send,
    last_recv,
    plane_send,
    plane_recv,
    up_send,
    up_recv,
    image_send,
    image_recv,
):
    freqs, bands, lateral, depth = dims
    n = bands // 2
    strip = lateral // bands
    rows = lateral // freqs
    tile = 2 * strip
    f = lax.axis_index("freq")
    b = lax.axis_index("band")
    x, y, l = lax.rem(f, n), lax.rem(f // n, n), f // (n * n)
    h, c = b // 2, lax.rem(b, 2)
    z = 2 * h + l
    home = lax.rem(h - y + n, n)
    number = l * n * n + y * n + home
    mine = 2 * x + c

    def at(xx, yy, zz, cc):
        return {"freq": (lax.rem(zz, 2) * n + yy) * n + xx, "band": (zz // 2) * 2 + cc}

    def wait_bytes(ref, sem):
        pltpu.make_async_copy(ref, ref, sem).wait()

    def remote(src, dst, send_sem, recv_sem, target):
        pltpu.make_async_remote_copy(
            src, dst, send_sem, recv_sem, device_id=target, device_id_type=MESH
        ).start()

    def send(src, dst, send_sem, recv_sem, target, here):
        @pl.when(jnp.logical_not(here))
        def _():
            remote(src, dst, send_sem, recv_sem, target)

        @pl.when(here)
        def _():
            pltpu.make_async_copy(src, dst, recv_sem).start()

    def loop(first, count, body):
        def step(i, carry):
            body(i)
            return carry

        lax.fori_loop(first, count, step, 0)

    def aligned(i, size):
        return pl.ds(pl.multiple_of(i * size, size), size)

    slab_load = pltpu.make_async_copy(slab_hbm.at[0], slab, slab_sem)
    table_load = pltpu.make_async_copy(table_hbm, table, table_sem)
    slab_load.start()
    barrier = pltpu.get_barrier_semaphore()

    def greet(axis, me, count):
        def body(d):
            pl.semaphore_signal(
                barrier, inc=1, device_id={axis: lax.rem(me + d, count)}, device_id_type=MESH
            )

        loop(1, count, body)

    greet("freq", f, freqs)
    greet("band", b, bands)
    loads = [
        pltpu.make_async_copy(
            wave.at[0, 2 * u + k], fields.at[u, :, pl.ds(k * strip, strip)], load_sem
        )
        for u in range(2)
        for k in range(2)
    ]
    for load in loads:
        load.start()
    table_load.start()
    slab_load.wait()
    chunk_tx[:, 0:rows, :] = (slab[...] - 1.0).astype(BF16).reshape(freqs, rows, strip)
    chunk_tx[:, rows:, :] = jnp.full((freqs, 16, strip), slot[0].astype(F32)).astype(BF16)
    pl.semaphore_wait(barrier, freqs + bands - 2)

    def send_chunk(d):
        g = lax.rem(f + d, freqs)
        remote(chunk_tx.at[g], chunk_rx.at[f], chunk_send, chunk_recv, {"freq": g})

    loop(1, freqs, send_chunk)
    pltpu.make_async_copy(chunk_tx.at[f], chunk_rx.at[f], chunk_recv).start()

    def omega_of(number):
        return OMEGA_LO + (OMEGA_HI - OMEGA_LO) * (number.astype(F32) + 0.5) / freqs

    omega = omega_of(slot[0])

    wait_bytes(chunk_rx, chunk_recv)
    for k in range(depth):
        select[k] = chunk_rx[owner[k], 0:rows, :]

    def send_slow(d):
        g = lax.rem(f + d, freqs)
        remote(select.at[0], slow.at[f], slow_send, slow_recv, {"freq": g})

    loop(1, freqs, send_slow)
    pltpu.make_async_copy(select.at[0], slow.at[f], slow_recv).start()

    def send_column(d):
        zz = lax.rem(z + d, bands)
        remote(
            select.at[pl.ds(1, depth - 1)],
            column.at[z],
            column_send,
            column_recv,
            at(x, y, zz, c),
        )

    loop(1, bands, send_column)
    pltpu.make_async_copy(select.at[pl.ds(1, depth - 1)], column.at[z], column_recv).start()

    def send_planes():
        wait_bytes(column, column_recv)

        def body(i):
            xx, yy = lax.rem(x + i // n, n), lax.rem(y + i, n)
            send(
                column.at[pl.ds(2 * xx, 2)],
                slow_mid.at[:, y * n + x],
                slow_mid_send,
                slow_mid_recv,
                at(xx, yy, z, c),
                i == 0,
            )

        loop(0, n * n, body)

    def omega_here():
        return omega_of(chunk_rx[number, rows : rows + 16, :])[0:1]

    def make_factor():
        omega_mid = omega_here()

        def body(i):
            shape = (strip, strip)
            kx = (lax.broadcasted_iota(jnp.int32, shape, 0) + (mine * strip + 1)).astype(F32)
            ky = (lax.broadcasted_iota(jnp.int32, shape, 1) + (i * strip + 1)).astype(F32)
            kx = math.pi * kx / (lateral + 1)
            ky = math.pi * ky / (lateral + 1)
            q = omega_mid * omega_mid - kx * kx - ky * ky
            theta = jnp.sqrt(jnp.maximum(q, 0.0))
            damp = jnp.exp(-jnp.sqrt(jnp.maximum(-q, 0.0)))
            factor[0, :, aligned(i, strip)] = damp * jnp.cos(theta)
            factor[1, :, aligned(i, strip)] = damp * jnp.sin(theta)

        loop(0, bands, body)

    def make_first_trig():
        def body(g):
            cosine, sine = small_cos_sin(omega * slow[g].astype(F32))
            trig[0, 0, aligned(g, rows)] = cosine
            trig[0, 1, aligned(g, rows)] = sine

        loop(0, freqs, body)

    def make_trig(step):
        omega_mid = omega_here()

        def body(g):
            value = slow_mid[g // (n * n), lax.rem(g, n * n), step - 1]
            cosine, sine = small_cos_sin(omega_mid * value.astype(F32))
            trig[step, 0, aligned(g, rows)] = cosine
            trig[step, 1, aligned(g, rows)] = sine

        loop(0, freqs, body)

    def hand(u):
        return -1.0 if u == 0 else 1.0

    def to_wavenumbers(step, u):
        def shift(block, value):
            cosine = trig[step, 0, block]
            sine = trig[step, 1, block] * hand(u)
            re = value[:, 0:strip]
            im = value[:, strip:]
            shifted[u, block, 0:strip] = (re * cosine - im * sine).astype(BF16)
            shifted[u, block, strip:] = (im * cosine + re * sine).astype(BF16)

        if step == 0:

            def first(i):
                block = aligned(i, strip)
                shift(block, fields[u, block])

            loop(0, bands, first)
        else:
            wait_bytes(prx.at[u], back_recv.at[u])

            def product_back(i):
                block = aligned(i, tile)
                value = jnp.dot(table[block, :], prx[u], preferred_element_type=F32)
                keep(step - 1, u, i, value)
                shift(block, value)

            loop(0, n, product_back)
            wait_bytes(tx.at[u, :, pl.ds(0, lateral - strip)], fwd_send.at[u])

        def product(i):
            t = lax.rem(x + 1 + i, n)
            block = aligned(t, tile)
            half = jnp.dot(table[block, :], shifted[u], preferred_element_type=F32).astype(BF16)
            tx[u, 0, block] = half[:, 0:strip]
            tx[u, 1, block] = half[:, strip:]
            for p in range(2):
                j = 2 * t + p
                if step == 0:
                    dst = mid.at[u, x, :, :, aligned(c, strip)]
                    sem = mid_recv.at[u, x]
                else:
                    dst = rx.at[u, :, :, aligned(mine, strip)]
                    sem = fwd_recv.at[u]
                send(
                    tx.at[u, :, aligned(j, strip)],
                    dst,
                    fwd_send.at[u],
                    sem,
                    at(t, y, z, p),
                    j == mine,
                )

        loop(0, n, product)

    def forward(u):
        def body(i):
            q = lax.rem(x + i, n)
            wait_bytes(mid.at[u, q], mid_recv.at[u, q])
            hh = lax.rem(q + y, n)
            send(
                mid.at[u, q],
                rx.at[u, :, :, aligned(h, tile)],
                mid_send.at[u],
                fwd_recv.at[u],
                at(x, y, 2 * hh + l, c),
                hh == h,
            )

        loop(0, n, body)

    def turn(step, u):
        def product(i):
            lanes = aligned(i, tile)
            lines = rx[u].reshape(2 * strip, lateral)
            spectrum = jnp.dot(lines, table[:, lanes], preferred_element_type=F32)
            re = spectrum[0:strip]
            im = spectrum[strip:]
            cosine = factor[0, :, lanes]
            sine = factor[1, :, lanes] * hand(u)
            turned[u, 0:strip, lanes] = (re * cosine - im * sine).astype(BF16)
            turned[u, strip:, lanes] = (im * cosine + re * sine).astype(BF16)

        loop(0, n, product)
        if step > 0:
            wait_bytes(ptx.at[u, pl.ds(0, bands - 1)], back_send.at[u])
        final = step == depth - 1

        def back(i):
            t = lax.rem((h if final else x) + 1 + i, n)
            lanes = aligned(t, tile)
            partial = jnp.dot(turned[u], table[:, lanes], preferred_element_type=F32).astype(BF16)
            for p in range(2):
                j = 2 * t + p
                cols = slice(p * strip, (p + 1) * strip)
                ptx[u, j, :, 0:strip] = partial[0:strip, cols]
                ptx[u, j, :, strip:] = partial[strip:, cols]
                block = aligned(mine, strip)
                if final:
                    send(
                        ptx.at[u, j],
                        last.at[u, block],
                        last_send.at[u],
                        last_recv.at[u],
                        at(home, y, 2 * t + l, p),
                        (home == x) & (j == b),
                    )
                else:
                    send(
                        ptx.at[u, j],
                        prx.at[u, block],
                        back_send.at[u],
                        back_recv.at[u],
                        at(t, y, z, p),
                        j == mine,
                    )

        loop(0, n, back)

    def to_fields(u):
        wait_bytes(last.at[u], last_recv.at[u])

        def product(i):
            block = aligned(i, tile)
            fields[u, block] = jnp.dot(table[block, :], last[u], preferred_element_type=F32)

        loop(0, n, product)

    normalizer = 1.0 / math.sqrt(freqs)

    def keep(step, u, i, value):
        block = aligned(i, tile)
        if u == 0:
            kept[block] = value
        else:
            term = kept[block] * value
            term = (term[:, 0:strip] + term[:, strip:]) * normalizer
            per = tile // rows
            start = i * per
            plane_tx[step, start // (n * n), pl.ds(lax.rem(start, n * n), per)] = term.astype(
                BF16
            ).reshape(per, rows, strip)

    def send_terms(step):
        def body_send(i):
            g = lax.rem(y * n + x + i, n * n)
            send(
                plane_tx.at[step, :, g],
                plane_rx.at[step, x, y],
                plane_send.at[step],
                plane_recv.at[step],
                at(lax.rem(g, n), g // n, z, c),
                i == 0,
            )

        loop(0, n * n, body_send)

    def send_sums(step):
        wait_bytes(plane_rx.at[step], plane_recv.at[step])

        def body(i):
            zz = lax.rem(z + i, bands)
            total = jnp.zeros((rows, strip), F32)
            for yy in range(n):
                total += plane_rx[step, zz // 2, yy, lax.rem(zz, 2)].astype(F32)
            column_tx[step, zz] = total.astype(BF16)
            send(
                column_tx.at[step, zz],
                column_rx.at[step, z],
                up_send.at[step],
                up_recv.at[step],
                at(x, y, zz, c),
                i == 0,
            )

        loop(0, bands, body)

    def send_image():
        def term(i):
            block = aligned(i, strip)
            value = fields[0, block] * fields[1, block]
            value = (value[:, 0:strip] + value[:, strip:]) * normalizer
            image_tx[block] = value.astype(BF16)

        loop(0, bands, term)

        def body(d):
            g = lax.rem(f + d, freqs)
            remote(
                image_tx.at[aligned(g, rows)], image_rx.at[f], image_send, image_recv, {"freq": g}
            )

        loop(1, freqs, body)
        pltpu.make_async_copy(image_tx.at[aligned(f, rows)], image_rx.at[f], image_recv).start()

    make_factor()
    for load in loads:
        load.wait()
    table_load.wait()
    wait_bytes(slow, slow_recv)
    make_first_trig()
    for u in range(2):
        to_wavenumbers(0, u)
    forward(0)
    send_planes()
    wait_bytes(rx.at[0], fwd_recv.at[0])
    forward(1)
    for step in range(depth):
        for u in range(2):
            if step > 0:
                to_wavenumbers(step, u)
        for u in range(2):
            if step > 0 or u > 0:
                wait_bytes(rx.at[u], fwd_recv.at[u])
            turn(step, u)
        if step == 0:
            wait_bytes(slow_mid, slow_mid_recv)
        if step < depth - 1:
            make_trig(step + 1)
    for step in range(depth - 1):
        send_terms(step)
    for step in range(depth - 1):
        send_sums(step)
    for u in range(2):
        to_fields(u)
    send_image()
    for u in range(2):
        for k in range(2):
            bottom[0, 2 * u + k] = fields[u, :, k * strip : (k + 1) * strip]

    for step in range(depth - 1):
        wait_bytes(column_rx.at[step], up_recv.at[step])
        image[step] = jnp.sum(column_rx[step].astype(F32), axis=0)
    wait_bytes(image_rx, image_recv)
    image[depth - 1] = jnp.sum(image_rx[...].astype(F32), axis=0)

    wait_bytes(chunk_tx.at[pl.ds(0, freqs - 1)], chunk_send)
    wait_bytes(slow.at[pl.ds(0, freqs - 1)], slow_send)
    wait_bytes(column.at[pl.ds(0, bands - 1)], column_send)
    wait_bytes(slow_mid.at[:, pl.ds(0, n * n - 1)], slow_mid_send)
    for u in range(2):
        wait_bytes(mid.at[u, pl.ds(0, n - 1)], mid_send.at[u])
        wait_bytes(tx.at[u, :, pl.ds(0, lateral - strip)], fwd_send.at[u])
        wait_bytes(ptx.at[u, pl.ds(0, bands - 1)], last_send.at[u])

        @pl.when(home != x)
        def _():
            wait_bytes(ptx.at[u, 0], last_send.at[u])

    for step in range(depth - 1):
        wait_bytes(plane_tx.at[step, :, pl.ds(0, n * n - 1)], plane_send.at[step])
        wait_bytes(column_tx.at[step, pl.ds(0, bands - 1)], up_send.at[step])
    wait_bytes(image_tx.at[pl.ds(0, lateral - rows)], image_send)


def body(wavefields, slowness_store, owner_plan, freq_slot):
    freqs = lax.axis_size("freq")
    bands = lax.axis_size("band")
    lateral = wavefields.shape[2]
    depth = owner_plan.shape[0]
    n = bands // 2
    strip = lateral // bands
    rows = lateral // freqs
    dims = (freqs, bands, lateral, depth)
    smem = pl.BlockSpec(memory_space=pltpu.SMEM)
    vmem = pl.BlockSpec(memory_space=pltpu.VMEM)
    hbm = pl.BlockSpec(memory_space=pltpu.HBM)
    dma = pltpu.SemaphoreType.DMA
    return pl.pallas_call(
        functools.partial(kernel, dims),
        out_shape=(
            jax.ShapeDtypeStruct((depth, rows, strip), F32),
            jax.ShapeDtypeStruct((1, 4, lateral, strip), F32),
        ),
        in_specs=[smem, smem, hbm, hbm, hbm],
        out_specs=(vmem, vmem),
        scratch_shapes=[
            pltpu.VMEM((lateral, lateral), BF16),
            pltpu.VMEM((lateral, strip), F32),
            pltpu.VMEM((2, lateral, 2 * strip), F32),
            pltpu.VMEM((2, lateral, 2 * strip), BF16),
            pltpu.VMEM((2, 2, lateral, strip), BF16),
            pltpu.VMEM((2, n, 2, strip, 2 * strip), BF16),
            pltpu.VMEM((2, 2, strip, lateral), BF16),
            pltpu.VMEM((2, 2 * strip, lateral), BF16),
            pltpu.VMEM((2, bands, strip, 2 * strip), BF16),
            pltpu.VMEM((2, lateral, 2 * strip), BF16),
            pltpu.VMEM((2, lateral, 2 * strip), BF16),
            pltpu.VMEM((depth, 2, lateral, strip), F32),
            pltpu.VMEM((2, strip, lateral), F32),
            pltpu.VMEM((freqs, rows + 16, strip), BF16),
            pltpu.VMEM((freqs, rows + 16, strip), BF16),
            pltpu.VMEM((depth, rows, strip), BF16),
            pltpu.VMEM((freqs, rows, strip), BF16),
            pltpu.VMEM((bands, depth - 1, rows, strip), BF16),
            pltpu.VMEM((2, n * n, depth - 1, rows, strip), BF16),
            pltpu.VMEM((lateral, 2 * strip), F32),
            pltpu.VMEM((depth - 1, 2, n * n, rows, strip), BF16),
            pltpu.VMEM((depth - 1, n, n, 2, rows, strip), BF16),
            pltpu.VMEM((depth - 1, bands, rows, strip), BF16),
            pltpu.VMEM((depth - 1, bands, rows, strip), BF16),
            pltpu.VMEM((lateral, strip), BF16),
            pltpu.VMEM((freqs, rows, strip), BF16),
            dma,
            dma,
            dma,
            dma,
            dma,
            dma,
            dma,
            dma,
            dma,
            dma,
            dma,
            dma((2,)),
            dma((2,)),
            dma((2,)),
            dma((2, n)),
            dma((2,)),
            dma((2,)),
            dma((2,)),
            dma((2,)),
            dma((depth - 1,)),
            dma((depth - 1,)),
            dma((depth - 1,)),
            dma((depth - 1,)),
            dma,
            dma,
        ],
        compiler_params=pltpu.CompilerParams(
            collective_id=0, has_side_effects=True, vmem_limit_bytes=36 * 2**20
        ),
    )(owner_plan, freq_slot, jnp.asarray(sine_table(lateral)), slowness_store, wavefields)


def solution(mesh):
    in_specs = (P("freq", None, None, "band"), P("freq", None, "band"), P(), P("freq"))
    out_specs = (P(None, "freq", "band"), P("freq", None, None, "band"))
    return jax.shard_map(body, mesh=mesh, in_specs=in_specs, out_specs=out_specs, check_vma=False)
```

```python
import functools
import math

import jax
import jax.numpy as jnp
import numpy as np
from jax import lax
from jax.experimental import pallas as pl
from jax.experimental.pallas import tpu as pltpu
from jax.sharding import PartitionSpec as P

OMEGA_LO = 1.5
OMEGA_HI = 3.0
MESH = pl.DeviceIdType.MESH
BF16 = jnp.bfloat16
F32 = jnp.float32


def sine_table(length):
    ordinal = np.arange(1, length + 1, dtype=np.int64)
    modulo = ordinal[:, None] * ordinal[None, :] % (2 * (length + 1))
    angles = math.pi * modulo / (length + 1)
    return (math.sqrt(2.0 / (length + 1)) * np.sin(angles)).astype(np.float32).astype(BF16)


def small_cos_sin(phi):
    p2 = phi * phi
    cosine = 1.0 + p2 * (-1 / 2 + p2 * (1 / 24 + p2 * (-1 / 720 + p2 * (1 / 40320))))
    sine = phi * (1.0 + p2 * (-1 / 6 + p2 * (1 / 120 + p2 * (-1 / 5040 + p2 * (1 / 362880)))))
    return cosine, sine


def kernel(
    dims,
    owner,
    slot,
    table_hbm,
    slab_hbm,
    wave,
    image,
    bottom,
    table,
    slab,
    fields,
    shifted,
    tx,
    mid,
    rx,
    turned,
    ptx,
    prx,
    last,
    trig,
    factor,
    chunk_tx,
    chunk_rx,
    slots_tx,
    slots,
    select,
    slow,
    column,
    slow_mid,
    kept,
    plane_tx,
    plane_rx,
    column_tx,
    column_rx,
    image_tx,
    image_rx,
    table_sem,
    slab_sem,
    load_sem,
    chunk_send,
    chunk_recv,
    slot_send,
    slot_recv,
    slow_send,
    slow_recv,
    column_send,
    column_recv,
    slow_mid_send,
    slow_mid_recv,
    fwd_send,
    fwd_recv,
    mid_send,
    mid_recv,
    back_send,
    back_recv,
    last_send,
    last_recv,
    plane_send,
    plane_recv,
    up_send,
    up_recv,
    image_send,
    image_recv,
):
    freqs, bands, lateral, depth = dims
    n = bands // 2
    strip = lateral // bands
    rows = lateral // freqs
    tile = 2 * strip
    f = lax.axis_index("freq")
    b = lax.axis_index("band")
    x, y, l = lax.rem(f, n), lax.rem(f // n, n), f // (n * n)
    h, c = b // 2, lax.rem(b, 2)
    z = 2 * h + l
    home = lax.rem(h - y + n, n)
    mine = 2 * x + c

    def at(xx, yy, zz, cc):
        return {"freq": (lax.rem(zz, 2) * n + yy) * n + xx, "band": (zz // 2) * 2 + cc}

    def wait_bytes(ref, sem):
        pltpu.make_async_copy(ref, ref, sem).wait()

    def remote(src, dst, send_sem, recv_sem, target):
        pltpu.make_async_remote_copy(
            src, dst, send_sem, recv_sem, device_id=target, device_id_type=MESH
        ).start()

    def send(src, dst, send_sem, recv_sem, target, here):
        @pl.when(jnp.logical_not(here))
        def _():
            remote(src, dst, send_sem, recv_sem, target)

        @pl.when(here)
        def _():
            pltpu.make_async_copy(src, dst, recv_sem).start()

    def loop(first, count, body):
        def step(i, carry):
            body(i)
            return carry

        lax.fori_loop(first, count, step, 0)

    def spread(i):
        return lax.rem(2 * i + i // 2, n) if n == 4 else i

    def aligned(i, size):
        return pl.ds(pl.multiple_of(i * size, size), size)

    slab_load = pltpu.make_async_copy(slab_hbm.at[0], slab, slab_sem)
    table_load = pltpu.make_async_copy(table_hbm, table, table_sem)
    slab_load.start()
    barrier = pltpu.get_barrier_semaphore()

    def greet(axis, me, count):
        def body(d):
            pl.semaphore_signal(
                barrier, inc=1, device_id={axis: lax.rem(me + d, count)}, device_id_type=MESH
            )

        loop(1, count, body)

    greet("freq", f, freqs)
    greet("band", b, bands)
    loads = [
        pltpu.make_async_copy(
            wave.at[0, 2 * u + k], fields.at[u, :, pl.ds(k * strip, strip)], load_sem
        )
        for u in range(2)
        for k in range(2)
    ]
    for load in loads:
        load.start()
    table_load.start()
    slab_load.wait()
    chunk_tx[...] = (slab[...] - 1.0).astype(BF16).reshape(freqs, rows, strip)
    slots_tx[...] = jnp.full((16, strip), slot[0].astype(F32)).astype(BF16)
    pl.semaphore_wait(barrier, freqs + bands - 2)

    def send_chunk(d):
        g = lax.rem(f + d, freqs)
        remote(chunk_tx.at[g], chunk_rx.at[f], chunk_send, chunk_recv, {"freq": g})

    loop(1, freqs, send_chunk)
    pltpu.make_async_copy(chunk_tx.at[f], chunk_rx.at[f], chunk_recv).start()

    def send_slot(d):
        remote(slots_tx, slots.at[x], slot_send, slot_recv, at(lax.rem(x + d, n), y, z, c))

    loop(1, n, send_slot)
    pltpu.make_async_copy(slots_tx, slots.at[x], slot_recv).start()

    def omega_of(number):
        return OMEGA_LO + (OMEGA_HI - OMEGA_LO) * (number.astype(F32) + 0.5) / freqs

    omega = omega_of(slot[0])

    wait_bytes(chunk_rx, chunk_recv)
    for k in range(depth):
        select[k] = chunk_rx[owner[k]]

    def send_slow(d):
        g = lax.rem(f + d, freqs)
        remote(select.at[0], slow.at[f], slow_send, slow_recv, {"freq": g})

    loop(1, freqs, send_slow)
    pltpu.make_async_copy(select.at[0], slow.at[f], slow_recv).start()

    def send_column(d):
        zz = lax.rem(z + d, bands)
        remote(
            select.at[pl.ds(1, depth - 1)],
            column.at[z],
            column_send,
            column_recv,
            at(x, y, zz, c),
        )

    loop(1, bands, send_column)
    pltpu.make_async_copy(select.at[pl.ds(1, depth - 1)], column.at[z], column_recv).start()

    def send_planes():
        wait_bytes(column, column_recv)

        def body(i):
            xx, yy = lax.rem(x + i // n, n), lax.rem(y + i, n)
            send(
                column.at[pl.ds(2 * xx, 2)],
                slow_mid.at[:, y * n + x],
                slow_mid_send,
                slow_mid_recv,
                at(xx, yy, z, c),
                i == 0,
            )

        loop(0, n * n, body)

    def omega_here():
        return omega_of(slots[home])[0:1]

    def make_factor():
        omega_mid = omega_here()

        def body(i):
            shape = (strip, strip)
            kx = (lax.broadcasted_iota(jnp.int32, shape, 0) + (mine * strip + 1)).astype(F32)
            ky = (lax.broadcasted_iota(jnp.int32, shape, 1) + (i * strip + 1)).astype(F32)
            kx = math.pi * kx / (lateral + 1)
            ky = math.pi * ky / (lateral + 1)
            q = omega_mid * omega_mid - kx * kx - ky * ky
            theta = jnp.sqrt(jnp.maximum(q, 0.0))
            damp = jnp.exp(-jnp.sqrt(jnp.maximum(-q, 0.0)))
            factor[0, :, aligned(i, strip)] = damp * jnp.cos(theta)
            factor[1, :, aligned(i, strip)] = damp * jnp.sin(theta)

        loop(0, bands, body)

    def make_trig(step):
        omega_mid = omega_here()

        def body(g):
            value = slow_mid[g // (n * n), lax.rem(g, n * n), step - 1]
            cosine, sine = small_cos_sin(omega_mid * value.astype(F32))
            trig[step, 0, aligned(g, rows)] = cosine
            trig[step, 1, aligned(g, rows)] = sine

        loop(0, freqs, body)

    def hand(u):
        return -1.0 if u == 0 else 1.0

    def to_wavenumbers(step, u):
        def shift(block, value):
            cosine = trig[step, 0, block]
            sine = trig[step, 1, block] * hand(u)
            re = value[:, 0:strip]
            im = value[:, strip:]
            shifted[u, block, 0:strip] = (re * cosine - im * sine).astype(BF16)
            shifted[u, block, strip:] = (im * cosine + re * sine).astype(BF16)

        if step == 0:

            def first(i):
                block = aligned(i, strip)
                if u == 0:
                    value = slow[aligned(i, strip // rows)].reshape(strip, strip)
                    cosine, sine = small_cos_sin(omega * value.astype(F32))
                    trig[0, 0, block] = cosine
                    trig[0, 1, block] = sine
                shift(block, fields[u, block])

            loop(0, bands, first)
        else:
            wait_bytes(prx.at[u], back_recv.at[u])

            def product_back(i):
                block = aligned(i, tile)
                value = jnp.dot(table[block, :], prx[u], preferred_element_type=F32)
                keep(step - 1, u, i, value)
                shift(block, value)

            loop(0, n, product_back)
            wait_bytes(tx.at[u, :, pl.ds(0, lateral - strip)], fwd_send.at[u])

        def product(i):
            t = lax.rem(x + spread(i if step == 0 else lax.rem(i + 1, n)), n)
            block = aligned(t, tile)
            half = jnp.dot(table[block, :], shifted[u], preferred_element_type=F32).astype(BF16)
            tx[u, 0, block] = half[:, 0:strip]
            tx[u, 1, block] = half[:, strip:]
            if step > 0 or u == 0:
                send_lines(step, u, t)

        loop(0, n, product)

    def send_lines(step, u, t):
        for p in range(2):
            j = 2 * t + p
            if step == 0:
                dst = mid.at[u, x, :, :, aligned(c, strip)]
                sem = mid_recv.at[u, x]
            else:
                dst = rx.at[u, :, :, aligned(mine, strip)]
                sem = fwd_recv.at[u]
            send(
                tx.at[u, :, aligned(j, strip)],
                dst,
                fwd_send.at[u],
                sem,
                at(t, y, z, p),
                j == mine,
            )

    def forward(u, i):
        q = lax.rem(x + spread(i), n)
        wait_bytes(mid.at[u, q], mid_recv.at[u, q])
        hh = lax.rem(q + y, n)
        send(
            mid.at[u, q],
            rx.at[u, :, :, aligned(h, tile)],
            mid_send.at[u],
            fwd_recv.at[u],
            at(x, y, 2 * hh + l, c),
            hh == h,
        )

    def turn(step, u):
        def product(i):
            lanes = aligned(i, tile)
            lines = rx[u].reshape(2 * strip, lateral)
            spectrum = jnp.dot(lines, table[:, lanes], preferred_element_type=F32)
            re = spectrum[0:strip]
            im = spectrum[strip:]
            cosine = factor[0, :, lanes]
            sine = factor[1, :, lanes] * hand(u)
            turned[u, 0:strip, lanes] = (re * cosine - im * sine).astype(BF16)
            turned[u, strip:, lanes] = (im * cosine + re * sine).astype(BF16)

        loop(0, n, product)
        if step > 0:
            wait_bytes(ptx.at[u, pl.ds(0, bands - 1)], back_send.at[u])
        final = step == depth - 1

        def back(i):
            t = lax.rem((h if final else x) + spread(lax.rem(i + 1, n)), n)
            lanes = aligned(t, tile)
            partial = jnp.dot(turned[u], table[:, lanes], preferred_element_type=F32).astype(BF16)
            for p in range(2):
                j = 2 * t + p
                cols = slice(p * strip, (p + 1) * strip)
                ptx[u, j, :, 0:strip] = partial[0:strip, cols]
                ptx[u, j, :, strip:] = partial[strip:, cols]
                block = aligned(mine, strip)
                if final:
                    send(
                        ptx.at[u, j],
                        last.at[u, block],
                        last_send.at[u],
                        last_recv.at[u],
                        at(home, y, 2 * t + l, p),
                        (home == x) & (j == b),
                    )
                else:
                    send(
                        ptx.at[u, j],
                        prx.at[u, block],
                        back_send.at[u],
                        back_recv.at[u],
                        at(t, y, z, p),
                        j == mine,
                    )

        loop(0, n, back)

    normalizer = 1.0 / math.sqrt(freqs)
    per = tile // rows

    def keep(step, u, i, value):
        block = aligned(i, tile)
        if u == 0:
            kept[block] = value
        else:
            term = kept[block] * value
            term = (term[:, 0:strip] + term[:, strip:]) * normalizer
            start = i * per
            plane_tx[step, start // (n * n), pl.ds(lax.rem(start, n * n), per)] = term.astype(
                BF16
            ).reshape(per, rows, strip)

    def send_terms(step):
        def body_send(i):
            g = lax.rem(y * n + x + i, n * n)
            send(
                plane_tx.at[step, :, g],
                plane_rx.at[step, x, y],
                plane_send.at[step],
                plane_recv.at[step],
                at(lax.rem(g, n), g // n, z, c),
                i == 0,
            )

        loop(0, n * n, body_send)

    def send_sums(step):
        wait_bytes(plane_rx.at[step], plane_recv.at[step])

        def body(i):
            zz = lax.rem(z + i, bands)
            total = jnp.zeros((rows, strip), F32)
            for yy in range(n):
                total += plane_rx[step, zz // 2, yy, lax.rem(zz, 2)].astype(F32)
            column_tx[step, zz] = total.astype(BF16)
            send(
                column_tx.at[step, zz],
                column_rx.at[step, z],
                up_send.at[step],
                up_recv.at[step],
                at(x, y, zz, c),
                i == 0,
            )

        loop(0, bands, body)

    def to_fields(u):
        wait_bytes(last.at[u], last_recv.at[u])

        def product(i):
            t = lax.rem(i + f // per, n)
            block = aligned(t, tile)
            value = jnp.dot(table[block, :], last[u], preferred_element_type=F32)
            bottom[0, 2 * u, block] = value[:, 0:strip]
            bottom[0, 2 * u + 1, block] = value[:, strip:]
            if u == 0:
                kept[block] = value
                return
            term = kept[block] * value
            term = (term[:, 0:strip] + term[:, strip:]) * normalizer
            image_tx[block] = term.astype(BF16)

            def body(k):
                g = t * per + k
                send(
                    image_tx.at[aligned(g, rows)],
                    image_rx.at[f],
                    image_send,
                    image_recv,
                    {"freq": g},
                    g == f,
                )

            loop(0, per, body)

        loop(0, n, product)

    wait_bytes(slots, slot_recv)
    make_factor()
    for load in loads:
        load.wait()
    table_load.wait()
    wait_bytes(slow, slow_recv)
    to_wavenumbers(0, 0)
    forward(0, 0)
    to_wavenumbers(0, 1)
    send_lines(0, 1, x)
    forward(1, 0)

    def alternate(i):
        forward(0, i)
        send_lines(0, 1, lax.rem(x + spread(i), n))

    loop(1, n, alternate)
    loop(1, n, functools.partial(forward, 1))
    send_planes()
    for step in range(depth):
        for u in range(2):
            if step > 0:
                to_wavenumbers(step, u)
        for u in range(2):
            wait_bytes(rx.at[u], fwd_recv.at[u])
            turn(step, u)
        if step == 0:
            wait_bytes(slow_mid, slow_mid_recv)
        if step < depth - 1:
            make_trig(step + 1)
    for step in range(depth - 1):
        send_terms(step)
    to_fields(0)
    for step in range(depth - 1):
        send_sums(step)
    to_fields(1)
    for step in range(depth - 1):
        wait_bytes(column_rx.at[step], up_recv.at[step])
        image[step] = jnp.sum(column_rx[step].astype(F32), axis=0)
    wait_bytes(image_rx, image_recv)
    image[depth - 1] = jnp.sum(image_rx[...].astype(F32), axis=0)

    wait_bytes(chunk_tx.at[pl.ds(0, freqs - 1)], chunk_send)
    wait_bytes(slots.at[pl.ds(0, n - 1)], slot_send)
    wait_bytes(slow.at[pl.ds(0, freqs - 1)], slow_send)
    wait_bytes(column.at[pl.ds(0, bands - 1)], column_send)
    wait_bytes(slow_mid.at[:, pl.ds(0, n * n - 1)], slow_mid_send)
    for u in range(2):
        wait_bytes(mid.at[u, pl.ds(0, n - 1)], mid_send.at[u])
        wait_bytes(tx.at[u, :, pl.ds(0, lateral - strip)], fwd_send.at[u])
        wait_bytes(ptx.at[u, pl.ds(0, bands - 1)], last_send.at[u])

        @pl.when(home != x)
        def _():
            wait_bytes(ptx.at[u, 0], last_send.at[u])

    for step in range(depth - 1):
        wait_bytes(plane_tx.at[step, :, pl.ds(0, n * n - 1)], plane_send.at[step])
        wait_bytes(column_tx.at[step, pl.ds(0, bands - 1)], up_send.at[step])
    wait_bytes(image_tx.at[pl.ds(0, lateral - rows)], image_send)


def body(wavefields, slowness_store, owner_plan, freq_slot):
    freqs = lax.axis_size("freq")
    bands = lax.axis_size("band")
    lateral = wavefields.shape[2]
    depth = owner_plan.shape[0]
    n = bands // 2
    strip = lateral // bands
    rows = lateral // freqs
    dims = (freqs, bands, lateral, depth)
    smem = pl.BlockSpec(memory_space=pltpu.SMEM)
    vmem = pl.BlockSpec(memory_space=pltpu.VMEM)
    hbm = pl.BlockSpec(memory_space=pltpu.HBM)
    dma = pltpu.SemaphoreType.DMA
    return pl.pallas_call(
        functools.partial(kernel, dims),
        out_shape=(
            jax.ShapeDtypeStruct((depth, rows, strip), F32),
            jax.ShapeDtypeStruct((1, 4, lateral, strip), F32),
        ),
        in_specs=[smem, smem, hbm, hbm, hbm],
        out_specs=(vmem, vmem),
        scratch_shapes=[
            pltpu.VMEM((lateral, lateral), BF16),
            pltpu.VMEM((lateral, strip), F32),
            pltpu.VMEM((2, lateral, 2 * strip), F32),
            pltpu.VMEM((2, lateral, 2 * strip), BF16),
            pltpu.VMEM((2, 2, lateral, strip), BF16),
            pltpu.VMEM((2, n, 2, strip, 2 * strip), BF16),
            pltpu.VMEM((2, 2, strip, lateral), BF16),
            pltpu.VMEM((2, 2 * strip, lateral), BF16),
            pltpu.VMEM((2, bands, strip, 2 * strip), BF16),
            pltpu.VMEM((2, lateral, 2 * strip), BF16),
            pltpu.VMEM((2, lateral, 2 * strip), BF16),
            pltpu.VMEM((depth, 2, lateral, strip), F32),
            pltpu.VMEM((2, strip, lateral), F32),
            pltpu.VMEM((freqs, rows, strip), BF16),
            pltpu.VMEM((freqs, rows, strip), BF16),
            pltpu.VMEM((16, strip), BF16),
            pltpu.VMEM((n, 16, strip), BF16),
            pltpu.VMEM((depth, rows, strip), BF16),
            pltpu.VMEM((freqs, rows, strip), BF16),
            pltpu.VMEM((bands, depth - 1, rows, strip), BF16),
            pltpu.VMEM((2, n * n, depth - 1, rows, strip), BF16),
            pltpu.VMEM((lateral, 2 * strip), F32),
            pltpu.VMEM((depth - 1, 2, n * n, rows, strip), BF16),
            pltpu.VMEM((depth - 1, n, n, 2, rows, strip), BF16),
            pltpu.VMEM((depth - 1, bands, rows, strip), BF16),
            pltpu.VMEM((depth - 1, bands, rows, strip), BF16),
            pltpu.VMEM((lateral, strip), BF16),
            pltpu.VMEM((freqs, rows, strip), BF16),
            dma,
            dma,
            dma,
            dma,
            dma,
            dma,
            dma,
            dma,
            dma,
            dma,
            dma,
            dma,
            dma,
            dma((2,)),
            dma((2,)),
            dma((2,)),
            dma((2, n)),
            dma((2,)),
            dma((2,)),
            dma((2,)),
            dma((2,)),
            dma((depth - 1,)),
            dma((depth - 1,)),
            dma((depth - 1,)),
            dma((depth - 1,)),
            dma,
            dma,
        ],
        compiler_params=pltpu.CompilerParams(
            collective_id=0, has_side_effects=True, vmem_limit_bytes=51 * 2**20
        ),
    )(owner_plan, freq_slot, jnp.asarray(sine_table(lateral)), slowness_store, wavefields)


def solution(mesh):
    in_specs = (P("freq", None, None, "band"), P("freq", None, "band"), P(), P("freq"))
    out_specs = (P(None, "freq", "band"), P("freq", None, None, "band"))
    return jax.shard_map(body, mesh=mesh, in_specs=in_specs, out_specs=out_specs, check_vma=False)
```

```python
import functools
import math

import jax
import jax.numpy as jnp
import numpy as np
from jax import lax
from jax.experimental import pallas as pl
from jax.experimental.pallas import tpu as pltpu
from jax.sharding import PartitionSpec as P

OMEGA_LO = 1.5
OMEGA_HI = 3.0
MESH = pl.DeviceIdType.MESH
BF16 = jnp.bfloat16
F32 = jnp.float32


def sine_table(length):
    ordinal = np.arange(1, length + 1, dtype=np.int64)
    modulo = ordinal[:, None] * ordinal[None, :] % (2 * (length + 1))
    angles = math.pi * modulo / (length + 1)
    return (math.sqrt(2.0 / (length + 1)) * np.sin(angles)).astype(np.float32).astype(BF16)


def small_cos_sin(phi):
    p2 = phi * phi
    cosine = 1.0 + p2 * (-1 / 2 + p2 * (1 / 24 + p2 * (-1 / 720 + p2 * (1 / 40320))))
    sine = phi * (1.0 + p2 * (-1 / 6 + p2 * (1 / 120 + p2 * (-1 / 5040 + p2 * (1 / 362880)))))
    return cosine, sine


def kernel(
    dims,
    owner,
    slot,
    table_hbm,
    slab_hbm,
    wave,
    image,
    bottom,
    table,
    slab,
    fields,
    shifted,
    tx,
    mid,
    rx,
    turned,
    ptx,
    prx,
    last,
    trig,
    factor,
    chunk_tx,
    chunk_rx,
    slots_tx,
    slots,
    select,
    slow,
    column,
    slow_mid,
    kept,
    plane_tx,
    plane_rx,
    column_tx,
    column_rx,
    image_tx,
    image_rx,
    table_sem,
    slab_sem,
    load_sem,
    chunk_send,
    chunk_recv,
    slot_send,
    slot_recv,
    slow_send,
    slow_recv,
    column_send,
    column_recv,
    slow_mid_send,
    slow_mid_recv,
    fwd_send,
    fwd_recv,
    mid_send,
    mid_recv,
    back_send,
    back_recv,
    last_send,
    last_recv,
    plane_send,
    plane_recv,
    up_send,
    up_recv,
    image_send,
    image_recv,
):
    freqs, bands, lateral, depth = dims
    n = bands // 2
    strip = lateral // bands
    rows = lateral // freqs
    tile = 2 * strip
    f = lax.axis_index("freq")
    b = lax.axis_index("band")
    x, y, l = lax.rem(f, n), lax.rem(f // n, n), f // (n * n)
    h, c = b // 2, lax.rem(b, 2)
    z = 2 * h + l
    home = lax.rem(h - y + n, n)
    mine = 2 * x + c

    def at(xx, yy, zz, cc):
        return {"freq": (lax.rem(zz, 2) * n + yy) * n + xx, "band": (zz // 2) * 2 + cc}

    def wait_bytes(ref, sem):
        pltpu.make_async_copy(ref, ref, sem).wait()

    def remote(src, dst, send_sem, recv_sem, target):
        pltpu.make_async_remote_copy(
            src, dst, send_sem, recv_sem, device_id=target, device_id_type=MESH
        ).start()

    def send(src, dst, send_sem, recv_sem, target, here):
        @pl.when(jnp.logical_not(here))
        def _():
            remote(src, dst, send_sem, recv_sem, target)

        @pl.when(here)
        def _():
            pltpu.make_async_copy(src, dst, recv_sem).start()

    def loop(first, count, body):
        def step(i, carry):
            body(i)
            return carry

        lax.fori_loop(first, count, step, 0)

    def spread(i):
        return lax.rem(2 * i + i // 2, n) if n == 4 else i

    def aligned(i, size):
        return pl.ds(pl.multiple_of(i * size, size), size)

    slab_load = pltpu.make_async_copy(slab_hbm.at[0], slab, slab_sem)
    table_load = pltpu.make_async_copy(table_hbm, table, table_sem)
    slab_load.start()
    barrier = pltpu.get_barrier_semaphore()

    def greet(axis, me, count):
        def body(d):
            pl.semaphore_signal(
                barrier, inc=1, device_id={axis: lax.rem(me + d, count)}, device_id_type=MESH
            )

        loop(1, count, body)

    greet("freq", f, freqs)
    greet("band", b, bands)
    loads = [
        pltpu.make_async_copy(
            wave.at[0, 2 * u + k], fields.at[u, :, pl.ds(k * strip, strip)], load_sem
        )
        for u in range(2)
        for k in range(2)
    ]
    for load in loads:
        load.start()
    table_load.start()
    slab_load.wait()
    chunk_tx[...] = (slab[...] - 1.0).astype(BF16).reshape(freqs, rows, strip)
    slots_tx[...] = jnp.full((16, strip), slot[0].astype(F32)).astype(BF16)
    pl.semaphore_wait(barrier, freqs + bands - 2)

    def send_chunk(d):
        g = lax.rem(f + d, freqs)
        remote(chunk_tx.at[g], chunk_rx.at[f], chunk_send, chunk_recv, {"freq": g})

    loop(1, freqs, send_chunk)
    pltpu.make_async_copy(chunk_tx.at[f], chunk_rx.at[f], chunk_recv).start()

    def send_slot(d):
        remote(slots_tx, slots.at[x], slot_send, slot_recv, at(lax.rem(x + d, n), y, z, c))

    loop(1, n, send_slot)
    pltpu.make_async_copy(slots_tx, slots.at[x], slot_recv).start()

    def omega_of(number):
        return OMEGA_LO + (OMEGA_HI - OMEGA_LO) * (number.astype(F32) + 0.5) / freqs

    omega = omega_of(slot[0])

    wait_bytes(chunk_rx, chunk_recv)
    for k in range(depth):
        select[k] = chunk_rx[owner[k]]

    def send_slow(d):
        g = lax.rem(f + d, freqs)
        remote(select.at[0], slow.at[f], slow_send, slow_recv, {"freq": g})

    loop(1, freqs, send_slow)
    pltpu.make_async_copy(select.at[0], slow.at[f], slow_recv).start()

    def send_column(d):
        zz = lax.rem(z + d, bands)
        remote(
            select.at[pl.ds(1, depth - 1)],
            column.at[z],
            column_send,
            column_recv,
            at(x, y, zz, c),
        )

    loop(1, bands, send_column)
    pltpu.make_async_copy(select.at[pl.ds(1, depth - 1)], column.at[z], column_recv).start()

    def send_planes():
        wait_bytes(column, column_recv)

        def body(i):
            xx, yy = lax.rem(x + i // n, n), lax.rem(y + i, n)
            send(
                column.at[pl.ds(2 * xx, 2)],
                slow_mid.at[:, y * n + x],
                slow_mid_send,
                slow_mid_recv,
                at(xx, yy, z, c),
                i == 0,
            )

        loop(0, n * n, body)

    def omega_here():
        return omega_of(slots[home])[0:1]

    def make_factor():
        omega_mid = omega_here()

        def body(i):
            shape = (strip, strip)
            kx = (lax.broadcasted_iota(jnp.int32, shape, 0) + (mine * strip + 1)).astype(F32)
            ky = (lax.broadcasted_iota(jnp.int32, shape, 1) + (i * strip + 1)).astype(F32)
            kx = math.pi * kx / (lateral + 1)
            ky = math.pi * ky / (lateral + 1)
            q = omega_mid * omega_mid - kx * kx - ky * ky
            theta = jnp.sqrt(jnp.maximum(q, 0.0))
            damp = jnp.exp(-jnp.sqrt(jnp.maximum(-q, 0.0)))
            factor[0, :, aligned(i, strip)] = damp * jnp.cos(theta)
            factor[1, :, aligned(i, strip)] = damp * jnp.sin(theta)

        loop(0, bands, body)

    def make_trig(step):
        omega_mid = omega_here()

        def body(g):
            value = slow_mid[g // (n * n), lax.rem(g, n * n), step - 1]
            cosine, sine = small_cos_sin(omega_mid * value.astype(F32))
            trig[step, 0, aligned(g, rows)] = cosine
            trig[step, 1, aligned(g, rows)] = sine

        loop(0, freqs, body)

    def hand(u):
        return -1.0 if u == 0 else 1.0

    def to_wavenumbers(step, u):
        def shift(block, value):
            cosine = trig[step, 0, block]
            sine = trig[step, 1, block] * hand(u)
            re = value[:, 0:strip]
            im = value[:, strip:]
            shifted[u, block, 0:strip] = (re * cosine - im * sine).astype(BF16)
            shifted[u, block, strip:] = (im * cosine + re * sine).astype(BF16)

        if step == 0:

            def first(i):
                block = aligned(i, strip)
                if u == 0:
                    value = slow[aligned(i, strip // rows)].reshape(strip, strip)
                    cosine, sine = small_cos_sin(omega * value.astype(F32))
                    trig[0, 0, block] = cosine
                    trig[0, 1, block] = sine
                shift(block, fields[u, block])

            loop(0, bands, first)
        else:
            wait_bytes(prx.at[u], back_recv.at[u])

            def product_back(i):
                block = aligned(i, tile)
                value = jnp.dot(table[block, :], prx[u], preferred_element_type=F32)
                keep(step - 1, u, i, value)
                shift(block, value)

            loop(0, n, product_back)
            wait_bytes(tx.at[u, :, pl.ds(0, lateral - strip)], fwd_send.at[u])

        def product(i):
            t = lax.rem(x + spread(i if step == 0 else lax.rem(i + 1, n)), n)
            block = aligned(t, tile)
            half = jnp.dot(table[block, :], shifted[u], preferred_element_type=F32).astype(BF16)
            tx[u, 0, block] = half[:, 0:strip]
            tx[u, 1, block] = half[:, strip:]
            if step > 0 or u == 0:
                send_lines(step, u, t)

        loop(0, n, product)

    def send_lines(step, u, t):
        for p in range(2):
            j = 2 * t + lax.rem(p + c, 2)
            if step == 0:
                dst = mid.at[u, x, :, :, aligned(c, strip)]
                sem = mid_recv.at[u, x]
            else:
                dst = rx.at[u, :, :, aligned(mine, strip)]
                sem = fwd_recv.at[u]
            send(
                tx.at[u, :, aligned(j, strip)],
                dst,
                fwd_send.at[u],
                sem,
                at(t, y, z, lax.rem(j, 2)),
                j == mine,
            )

    def forward(u, i):
        q = lax.rem(x + spread(i), n)
        wait_bytes(mid.at[u, q], mid_recv.at[u, q])
        hh = lax.rem(q + y, n)
        send(
            mid.at[u, q],
            rx.at[u, :, :, aligned(h, tile)],
            mid_send.at[u],
            fwd_recv.at[u],
            at(x, y, 2 * hh + l, c),
            hh == h,
        )

    def turn(step, u):
        def product(i):
            lanes = aligned(i, tile)
            lines = rx[u].reshape(2 * strip, lateral)
            spectrum = jnp.dot(lines, table[:, lanes], preferred_element_type=F32)
            re = spectrum[0:strip]
            im = spectrum[strip:]
            cosine = factor[0, :, lanes]
            sine = factor[1, :, lanes] * hand(u)
            turned[u, 0:strip, lanes] = (re * cosine - im * sine).astype(BF16)
            turned[u, strip:, lanes] = (im * cosine + re * sine).astype(BF16)

        loop(0, n, product)
        if step > 0:
            wait_bytes(ptx.at[u, pl.ds(0, bands - 1)], back_send.at[u])
        final = step == depth - 1

        def back(i):
            t = lax.rem((h if final else x) + spread(lax.rem(i + 1, n)), n)
            lanes = aligned(t, tile)
            partial = jnp.dot(turned[u], table[:, lanes], preferred_element_type=F32).astype(BF16)
            for p in range(2):
                j = 2 * t + p
                cols = slice(p * strip, (p + 1) * strip)
                ptx[u, j, :, 0:strip] = partial[0:strip, cols]
                ptx[u, j, :, strip:] = partial[strip:, cols]
            for p in range(2):
                core = lax.rem(p + c, 2)
                j = 2 * t + core
                block = aligned(mine, strip)
                if final:
                    send(
                        ptx.at[u, j],
                        last.at[u, block],
                        last_send.at[u],
                        last_recv.at[u],
                        at(home, y, 2 * t + l, core),
                        (home == x) & (j == b),
                    )
                else:
                    send(
                        ptx.at[u, j],
                        prx.at[u, block],
                        back_send.at[u],
                        back_recv.at[u],
                        at(t, y, z, core),
                        j == mine,
                    )

        loop(0, n, back)

    normalizer = 1.0 / math.sqrt(freqs)
    per = tile // rows

    def keep(step, u, i, value):
        block = aligned(i, tile)
        if u == 0:
            kept[block] = value
        else:
            term = kept[block] * value
            term = (term[:, 0:strip] + term[:, strip:]) * normalizer
            start = i * per
            plane_tx[step, start // (n * n), pl.ds(lax.rem(start, n * n), per)] = term.astype(
                BF16
            ).reshape(per, rows, strip)

    def send_terms(step):
        def body_send(i):
            g = lax.rem(y * n + x + i, n * n)
            send(
                plane_tx.at[step, :, g],
                plane_rx.at[step, x, y],
                plane_send.at[step],
                plane_recv.at[step],
                at(lax.rem(g, n), g // n, z, c),
                i == 0,
            )

        loop(0, n * n, body_send)

    def send_sums(step):
        wait_bytes(plane_rx.at[step], plane_recv.at[step])

        def body(i):
            zz = lax.rem(z + i, bands)
            total = jnp.zeros((rows, strip), F32)
            for yy in range(n):
                total += plane_rx[step, zz // 2, yy, lax.rem(zz, 2)].astype(F32)
            column_tx[step, zz] = total.astype(BF16)
            send(
                column_tx.at[step, zz],
                column_rx.at[step, z],
                up_send.at[step],
                up_recv.at[step],
                at(x, y, zz, c),
                i == 0,
            )

        loop(0, bands, body)

    def to_fields(u):
        wait_bytes(last.at[u], last_recv.at[u])

        def product(i):
            t = lax.rem(i + f // per, n)
            block = aligned(t, tile)
            value = jnp.dot(table[block, :], last[u], preferred_element_type=F32)
            bottom[0, 2 * u, block] = value[:, 0:strip]
            bottom[0, 2 * u + 1, block] = value[:, strip:]
            if u == 0:
                kept[block] = value
                return
            term = kept[block] * value
            term = (term[:, 0:strip] + term[:, strip:]) * normalizer
            image_tx[block] = term.astype(BF16)

            def body(k):
                g = t * per + k
                send(
                    image_tx.at[aligned(g, rows)],
                    image_rx.at[f],
                    image_send,
                    image_recv,
                    {"freq": g},
                    g == f,
                )

            loop(0, per, body)

        loop(0, n, product)

    for load in loads:
        load.wait()
    table_load.wait()
    wait_bytes(slow, slow_recv)
    to_wavenumbers(0, 0)
    forward(0, 0)
    to_wavenumbers(0, 1)
    send_lines(0, 1, x)
    forward(1, 0)

    def alternate(i):
        forward(0, i)
        send_lines(0, 1, lax.rem(x + spread(i), n))

    loop(1, n, alternate)
    loop(1, n, functools.partial(forward, 1))
    send_planes()
    wait_bytes(slots, slot_recv)
    make_factor()
    for step in range(depth):
        for u in range(2):
            if step > 0:
                to_wavenumbers(step, u)
        for u in range(2):
            wait_bytes(rx.at[u], fwd_recv.at[u])
            turn(step, u)
        if step == 0:
            wait_bytes(slow_mid, slow_mid_recv)
        if step < depth - 1:
            make_trig(step + 1)
    for step in range(depth - 1):
        send_terms(step)
    to_fields(0)
    for step in range(depth - 1):
        send_sums(step)
    to_fields(1)
    for step in range(depth - 1):
        wait_bytes(column_rx.at[step], up_recv.at[step])
        image[step] = jnp.sum(column_rx[step].astype(F32), axis=0)
    wait_bytes(image_rx, image_recv)
    image[depth - 1] = jnp.sum(image_rx[...].astype(F32), axis=0)

    wait_bytes(chunk_tx.at[pl.ds(0, freqs - 1)], chunk_send)
    wait_bytes(slots.at[pl.ds(0, n - 1)], slot_send)
    wait_bytes(slow.at[pl.ds(0, freqs - 1)], slow_send)
    wait_bytes(column.at[pl.ds(0, bands - 1)], column_send)
    wait_bytes(slow_mid.at[:, pl.ds(0, n * n - 1)], slow_mid_send)
    for u in range(2):
        wait_bytes(mid.at[u, pl.ds(0, n - 1)], mid_send.at[u])
        wait_bytes(tx.at[u, :, pl.ds(0, lateral - strip)], fwd_send.at[u])
        wait_bytes(ptx.at[u, pl.ds(0, bands - 1)], last_send.at[u])

        @pl.when(home != x)
        def _():
            wait_bytes(ptx.at[u, 0], last_send.at[u])

    for step in range(depth - 1):
        wait_bytes(plane_tx.at[step, :, pl.ds(0, n * n - 1)], plane_send.at[step])
        wait_bytes(column_tx.at[step, pl.ds(0, bands - 1)], up_send.at[step])
    wait_bytes(image_tx.at[pl.ds(0, lateral - rows)], image_send)


def body(wavefields, slowness_store, owner_plan, freq_slot):
    freqs = lax.axis_size("freq")
    bands = lax.axis_size("band")
    lateral = wavefields.shape[2]
    depth = owner_plan.shape[0]
    n = bands // 2
    strip = lateral // bands
    rows = lateral // freqs
    dims = (freqs, bands, lateral, depth)
    smem = pl.BlockSpec(memory_space=pltpu.SMEM)
    vmem = pl.BlockSpec(memory_space=pltpu.VMEM)
    hbm = pl.BlockSpec(memory_space=pltpu.HBM)
    dma = pltpu.SemaphoreType.DMA
    return pl.pallas_call(
        functools.partial(kernel, dims),
        out_shape=(
            jax.ShapeDtypeStruct((depth, rows, strip), F32),
            jax.ShapeDtypeStruct((1, 4, lateral, strip), F32),
        ),
        in_specs=[smem, smem, hbm, hbm, hbm],
        out_specs=(vmem, vmem),
        scratch_shapes=[
            pltpu.VMEM((lateral, lateral), BF16),
            pltpu.VMEM((lateral, strip), F32),
            pltpu.VMEM((2, lateral, 2 * strip), F32),
            pltpu.VMEM((2, lateral, 2 * strip), BF16),
            pltpu.VMEM((2, 2, lateral, strip), BF16),
            pltpu.VMEM((2, n, 2, strip, 2 * strip), BF16),
            pltpu.VMEM((2, 2, strip, lateral), BF16),
            pltpu.VMEM((2, 2 * strip, lateral), BF16),
            pltpu.VMEM((2, bands, strip, 2 * strip), BF16),
            pltpu.VMEM((2, lateral, 2 * strip), BF16),
            pltpu.VMEM((2, lateral, 2 * strip), BF16),
            pltpu.VMEM((depth, 2, lateral, strip), F32),
            pltpu.VMEM((2, strip, lateral), F32),
            pltpu.VMEM((freqs, rows, strip), BF16),
            pltpu.VMEM((freqs, rows, strip), BF16),
            pltpu.VMEM((16, strip), BF16),
            pltpu.VMEM((n, 16, strip), BF16),
            pltpu.VMEM((depth, rows, strip), BF16),
            pltpu.VMEM((freqs, rows, strip), BF16),
            pltpu.VMEM((bands, depth - 1, rows, strip), BF16),
            pltpu.VMEM((2, n * n, depth - 1, rows, strip), BF16),
            pltpu.VMEM((lateral, 2 * strip), F32),
            pltpu.VMEM((depth - 1, 2, n * n, rows, strip), BF16),
            pltpu.VMEM((depth - 1, n, n, 2, rows, strip), BF16),
            pltpu.VMEM((depth - 1, bands, rows, strip), BF16),
            pltpu.VMEM((depth - 1, bands, rows, strip), BF16),
            pltpu.VMEM((lateral, strip), BF16),
            pltpu.VMEM((freqs, rows, strip), BF16),
            dma,
            dma,
            dma,
            dma,
            dma,
            dma,
            dma,
            dma,
            dma,
            dma,
            dma,
            dma,
            dma,
            dma((2,)),
            dma((2,)),
            dma((2,)),
            dma((2, n)),
            dma((2,)),
            dma((2,)),
            dma((2,)),
            dma((2,)),
            dma((depth - 1,)),
            dma((depth - 1,)),
            dma((depth - 1,)),
            dma((depth - 1,)),
            dma,
            dma,
        ],
        compiler_params=pltpu.CompilerParams(
            collective_id=0, has_side_effects=True, vmem_limit_bytes=51 * 2**20
        ),
    )(owner_plan, freq_slot, jnp.asarray(sine_table(lateral)), slowness_store, wavefields)


def solution(mesh):
    in_specs = (P("freq", None, None, "band"), P("freq", None, "band"), P(), P("freq"))
    out_specs = (P(None, "freq", "band"), P("freq", None, None, "band"))
    return jax.shard_map(body, mesh=mesh, in_specs=in_specs, out_specs=out_specs, check_vma=False)
```
